256 devices in a mesh: rep: 8 (over x, z_hi), zero: 32 (over z_lo, y, core).
Axes of the slice: x: 4, y: 4, z: 8 (z_hi: 2, z_lo: 4; z = z_hi * 4 + z_lo), core: 2. Of those that a mesh axis runs over, the one named last changes fastest.
Arguments:
- gated_input: bfloat16 [8, 4096, 4096], P('rep', 'zero'), may hold values from -6 to 6
- query_gate: bfloat16 [8, 4096, 4096], P('rep', 'zero'), may hold values from -12 to 12
- cotangent: bfloat16 [8, 4096, 4096], P('rep', 'zero'), may hold values from -8 to 8
- filters: float32 [8, 256, 128], P('rep', 'zero'), may hold values from -0.5 to 0.5
- first_moment: float32 [8, 256, 128], P('rep', 'zero'), may hold values from -0.03125 to 0.03125
- second_moment: float32 [8, 256, 128], P('rep', 'zero'), may hold values from 1e-06 to 0.0001
- step_index: int32 [1], replicated, may hold values from 0 to 999
Outputs:
- query_grad: bfloat16 [8, 4096, 4096], P('rep', 'zero')
- input_grad: bfloat16 [8, 4096, 4096], P('rep', 'zero')
- new_filters: float32 [8, 256, 128], P('rep', 'zero')
The draws below stay inside these ranges and needn't reach their ends.
All inputs are finite; a program needn't handle non-finite values.
Results may differ from the reference program's by a relative error of at most 0.007.
Values may be sent and summed in bfloat16 or wider, within the bound.
A program may use at most 256 MiB of HBM per device.

```python
import math
import jax
import jax.numpy as jnp
from jax import lax

C = 4096
GS = 16
K = 128
G = 256
TOKENS = 4096
REPS = 8
N_REP = 8


def draw_query_gate(key, part):
    channel_pos = jnp.arange(C).astype(jnp.float32) / C
    scale_row = 0.3 * jnp.exp(jnp.log(10.0) * channel_pos)
    base = jnp.clip(jax.random.normal(key, (REPS, TOKENS, C), jnp.float32), -4.0, 4.0)
    return (base * scale_row[None, None, :]).astype(jnp.bfloat16)


def draw_cotangent(key, part):
    position = jnp.arange(TOKENS).astype(jnp.float32) / TOKENS
    scale_col = 0.6 * jnp.exp(jnp.log(3.0) * position)
    base = jnp.clip(jax.random.normal(key, (REPS, TOKENS, C), jnp.float32), -4.0, 4.0)
    return (base * scale_col[None, :, None]).astype(jnp.bfloat16)


def level_of(stream_key, dims, split, low, top_value):
    loudness, own = 1.0, jax.random.fold_in(stream_key, 6)
    for dim, parts in split:
        draws = jnp.exp(jax.random.uniform(jax.random.fold_in(own, dim), (parts,), jnp.float32, low / len(split), top_value / len(split)))
        loudness = loudness * jnp.repeat(draws, dims[dim] // parts).reshape([-1 if axis == dim else 1 for axis in range(len(dims))])
    return loudness


def gaussian(key, shape, scale, limit, cuts=(), held_as=jnp.bfloat16):
    entries = jax.random.normal(key, shape, jnp.float32) * scale
    if len(cuts) > 0:
        entries = level_of(key, shape, cuts, -0.22, 0.18) * entries
    return jnp.clip(entries, min=-limit, max=limit).astype(held_as)


def setup_inputs(seed: int = 0) -> dict:
    keys = jax.random.split(jax.random.key(seed), 8)
    gated_input = gaussian(keys[0], (REPS, TOKENS, C), 1.0, 6.0, ((0, 8), (1, 32)))
    query_gate = draw_query_gate(jax.random.fold_in(keys[7], 71), 0)
    cotangent = draw_cotangent(jax.random.fold_in(keys[7], 71), 0)
    filters = gaussian(keys[3], (REPS, G, K), K ** -0.5, 0.5, ((0, 8), (1, 32)), jnp.float32)
    first_moment = gaussian(keys[4], (REPS, G, K), 0.005, 0.03125, ((0, 8), (1, 32)), jnp.float32)
    second_moment = jnp.clip(jnp.exp(math.log(0.0001) - 4.6051702 * jax.random.uniform(keys[5], (REPS, G, K), jnp.float32) ** level_of(keys[5], (REPS, G, K), ((0, 8), (1, 32)), -0.2, 0.2)), 9.999999974752427e-07, 0.0001)
    step_index = jax.random.randint(keys[6], (1,), 0, 1000).astype(jnp.int32)
    return dict(gated_input=gated_input, query_gate=query_gate, cotangent=cotangent, filters=filters, first_moment=first_moment, second_moment=second_moment, step_index=step_index)


CLIP_NORM = 1.0
BETA_ONE = 0.9
BETA_TWO = 0.95
LEARN_RATE = 0.05
ADAM_EPS = 1e-08

def one_group(operands):
    inputs, gate_values, upstream, filter_row = operands
    length = 2 * TOKENS
    inputs_wide = inputs.astype(jnp.float32)
    upstream_wide = upstream.astype(jnp.float32)
    mixed_half = (upstream_wide * gate_values.astype(jnp.float32)).astype(jnp.bfloat16)
    mixed_half = lax.optimization_barrier(mixed_half)
    mixed_rows = mixed_half.astype(jnp.float32)
    per_channel = jnp.repeat(filter_row.astype(jnp.float32), GS, axis=0).T
    spec_input = jnp.fft.rfft(inputs_wide, length, axis=0)
    spec_filter = jnp.fft.rfft(per_channel, length, axis=0)
    spec_mixed = jnp.fft.rfft(mixed_rows, length, axis=0)
    conv_out = jnp.fft.irfft(spec_input * spec_filter, length, axis=0)[:TOKENS]
    query_grad = (upstream_wide * conv_out).astype(jnp.bfloat16)
    input_grad = jnp.fft.irfft(spec_mixed * jnp.conj(spec_filter), length, axis=0)[:TOKENS].astype(jnp.bfloat16)
    lagged = jnp.fft.irfft(spec_mixed * jnp.conj(spec_input), length, axis=0)[:K]
    grad = lagged.reshape(K, C // GS, GS).sum(axis=2).T
    return (query_grad, input_grad, grad.astype(jnp.float32))

def reference(gated_input, query_gate, cotangent, filters, first_moment, second_moment, step_index):
    half_filters = filters.astype(jnp.bfloat16)
    query_grad, input_grad, grads = lax.map(one_group, (gated_input, query_gate, cotangent, half_filters))
    norm_value = jnp.sqrt(lax.optimization_barrier(jnp.sum(grads * grads, axis=(1, 2))))
    clip_scale = jnp.minimum(1.0, CLIP_NORM / (norm_value + 1e-06))
    clipped = grads * clip_scale[:, None, None]
    step_count = step_index[0].astype(jnp.float32) + 1.0
    moment_one = BETA_ONE * first_moment + (1.0 - BETA_ONE) * clipped
    moment_two = BETA_TWO * second_moment + (1.0 - BETA_TWO) * clipped * clipped
    corrected_one = moment_one / (1.0 - jnp.power(BETA_ONE, step_count))
    corrected_two = moment_two / (1.0 - jnp.power(BETA_TWO, step_count))
    stepped = filters - LEARN_RATE * corrected_one / (jnp.sqrt(corrected_two) + ADAM_EPS)
    bit_count = N_REP.bit_length() - 1
    partner_bit = step_index[0] % bit_count
    partners = jnp.bitwise_xor(jnp.arange(N_REP, dtype=jnp.int32), jnp.left_shift(jnp.int32(1), partner_bit))
    new_filters = 0.5 * (stepped + stepped[partners])
    return (query_grad, input_grad, new_filters)
```

```python
import math

import jax
import jax.numpy as jnp
from jax import lax
from jax.experimental import pallas as pl
from jax.experimental.pallas import tpu as pltpu
from jax.sharding import PartitionSpec as P

CLIP_NORM = 1.0
BETA_ONE = 0.9
BETA_TWO = 0.95
LEARN_RATE = 0.05
ADAM_EPS = 1e-08

BF = jnp.bfloat16
F32 = jnp.float32
MESH = pl.DeviceIdType.MESH

ZERO = 32
CHUNKS = 8
TILES = 4
HALF = CHUNKS // 2
WIDE = TILES * 128
GROUPS = TILES * 8


def lane_ids():
    return lax.broadcasted_iota(jnp.int32, (16, 128), 1)


def row_ids():
    return lax.broadcasted_iota(jnp.int32, (16, 128), 0)


def exchange(blocks):
    part = lane_ids() // 16
    r = [blocks[0]] + [pltpu.roll(blocks[a], 16 * a, 1) for a in range(1, 8)]
    for s in (1, 2, 4):
        pick = (part & s) != 0
        r = [jnp.where(pick, r[(i + s) % 8], r[i]) for i in range(8)]
    return [r[0]] + [pltpu.roll(r[8 - g], 128 - 16 * g, 1) for g in range(1, 8)]


def windows(low, high):
    lanes = lane_ids()
    out = [low]
    for q in range(1, 8):
        out.append(pltpu.roll(jnp.where(lanes >= 16 * q, low, high), 128 - 16 * q, 1))
    return out + [high]


def forward_taps(row):
    taps = jnp.take_along_axis(
        jnp.broadcast_to(row, (16, 128)), (row_ids() - lane_ids()) & 127, axis=1
    )
    keep = lane_ids() > row_ids()
    none = jnp.zeros_like(taps)
    first, last = jnp.where(keep, taps, none), jnp.where(keep, none, taps)
    return jnp.concatenate([first, last[:, :16]], axis=1).astype(BF)


def backward_taps(row):
    taps = jnp.take_along_axis(
        jnp.broadcast_to(row, (16, 128)), (lane_ids() - row_ids()) & 127, axis=1
    )
    keep = lane_ids() >= row_ids()
    none = jnp.zeros_like(taps)
    first, last = jnp.where(keep, taps, none), jnp.where(keep, none, taps)
    return jnp.concatenate([first, last[:, :16]], axis=1).astype(BF)


def pair_convolved(taps_two, wins_two):
    taps = jnp.concatenate(taps_two, axis=0)
    wins = jnp.concatenate(
        [jnp.concatenate([u, v], axis=1) for u, v in zip(*wins_two)], axis=0
    )
    out = jnp.dot(taps, wins, preferred_element_type=F32)
    return [out[:16, :128].astype(BF), out[16:, 128:].astype(BF)]


def pair_lags(own_two, wins_two):
    none = jnp.zeros((16, 128), BF)
    rows = jnp.concatenate(
        [jnp.concatenate([own_two[0], none], 1), jnp.concatenate([none, own_two[1]], 1)], 0
    )
    wins = jnp.concatenate(
        [jnp.concatenate([u, v], axis=1) for u, v in zip(*wins_two)], axis=0
    )
    out = lax.dot_general(rows, wins, (((1,), (1,)), ((), ())), preferred_element_type=F32)
    return [out[:16], out[16:]]


def diagonal(lag, forward):
    tail = jnp.concatenate([lag[:, 128:144], jnp.zeros((16, 112), F32)], axis=1)
    if forward:
        keep, index = lane_ids() > row_ids(), (row_ids() - lane_ids()) & 127
    else:
        keep, index = lane_ids() >= row_ids(), (lane_ids() + row_ids()) & 127
    turned = jnp.take_along_axis(jnp.where(keep, lag[:, :128], tail), index, axis=1)
    return turned[:8] + turned[8:]


def kernel(
    x_hbm,
    gate_hbm,
    ct_hbm,
    filt_ref,
    one_ref,
    two_ref,
    step_ref,
    qg_hbm,
    ig_hbm,
    new_ref,
    x_in,
    gate_in,
    ct_in,
    x_own,
    m_own,
    x_prev,
    m_next,
    taps,
    grads,
    shares,
    squares,
    stepped,
    partners,
    qg,
    ig,
    x_ld,
    gate_ld,
    ct_ld,
    x_snd,
    x_rcv,
    m_snd,
    m_rcv,
    f_snd,
    f_rcv,
    g_snd,
    g_rcv,
    s_snd,
    s_rcv,
    p_snd,
    p_rcv,
    qg_st,
    ig_st,
):
    me = lax.axis_index("zero")
    rep = lax.axis_index("rep")
    has_next = me < ZERO - 1
    has_prev = me > 0
    mates = [
        rep + 1 - 2 * lax.rem(rep, 2),
        rep + 2 - 4 * lax.rem(lax.div(rep, 2), 2),
        lax.rem(rep + 4, 8),
    ]

    def ahead(d):
        return lax.rem(me + d, ZERO)

    def behind(d):
        return lax.rem(me + ZERO - d, ZERO)

    barrier = pltpu.get_barrier_semaphore()

    @pl.loop(1, ZERO)
    def _(d):
        pl.semaphore_signal(barrier, 1, device_id={"zero": ahead(d)}, device_id_type=MESH)

    for mate in mates:
        pl.semaphore_signal(barrier, 1, device_id={"rep": mate}, device_id_type=MESH)

    def wide(i):
        return pl.ds(pl.multiple_of(i * WIDE, WIDE), WIDE)

    def load(hbm, vmem, sem, i):
        return pltpu.make_async_copy(hbm.at[0, :, wide(i)], vmem.at[:, wide(i)], sem.at[i])

    @pl.loop(0, CHUNKS)
    def _(i):
        load(x_hbm, x_in, x_ld, i).start()
        load(ct_hbm, ct_in, ct_ld, CHUNKS - 1 - i).start()
        load(gate_hbm, gate_in, gate_ld, CHUNKS - 1 - i).start()

    @pl.when(me == 0)
    def _():
        x_prev[...] = jnp.zeros_like(x_prev)

    @pl.when(me == ZERO - 1)
    def _():
        m_next[...] = jnp.zeros_like(m_next)

    def slab(i):
        return pl.ds(i * GROUPS, GROUPS)

    def x_copy(i):
        return pltpu.make_async_remote_copy(
            src_ref=x_own.at[slab(i)],
            dst_ref=x_prev.at[slab(i)],
            send_sem=x_snd.at[i],
            recv_sem=x_rcv.at[i],
            device_id={"zero": ahead(1)},
            device_id_type=MESH,
        )

    def m_copy(i):
        return pltpu.make_async_remote_copy(
            src_ref=m_own.at[slab(i)],
            dst_ref=m_next.at[slab(i)],
            send_sem=m_snd.at[i],
            recv_sem=m_rcv.at[i],
            device_id={"zero": behind(1)},
            device_id_type=MESH,
        )

    def tile_of(t):
        return pl.ds(pl.multiple_of(t * 128, 128), 128)

    def arrange_x(i):
        load(x_hbm, x_in, x_ld, i).wait()
        for u in range(TILES):
            t = i * TILES + u
            out = exchange([x_in[16 * a : 16 * a + 16, tile_of(t)] for a in range(8)])
            for g in range(8):
                x_own[t * 8 + g] = out[g]

    def arrange_m(i):
        load(ct_hbm, ct_in, ct_ld, i).wait()
        load(gate_hbm, gate_in, gate_ld, i).wait()
        for u in range(TILES):
            t = i * TILES + u
            mixed = [
                (
                    ct_in[16 * a : 16 * a + 16, tile_of(t)].astype(F32)
                    * gate_in[16 * a : 16 * a + 16, tile_of(t)].astype(F32)
                ).astype(BF)
                for a in range(8)
            ]
            out = exchange(mixed)
            for g in range(8):
                m_own[t * 8 + g] = out[g]

    def send_x(i):
        @pl.when(has_next)
        def _():
            x_copy(i).start()

    def send_m(i):
        @pl.when(has_prev)
        def _():
            m_copy(i).start()

    def to_peer(src, dst, snd, rcv, d):
        return pltpu.make_async_remote_copy(
            src_ref=src,
            dst_ref=dst,
            send_sem=snd.at[d],
            recv_sem=rcv.at[d],
            device_id={"zero": ahead(d)},
            device_id_type=MESH,
        )

    arrange_x(0)
    pl.semaphore_wait(barrier, ZERO - 1 + len(mates))
    send_x(0)
    arrange_m(CHUNKS - 1)
    send_m(CHUNKS - 1)

    @pl.loop(1, ZERO)
    def _(d):
        to_peer(filt_ref.at[0], taps.at[me], f_snd, f_rcv, d).start()

    taps[me] = filt_ref[0]

    @pl.loop(1, CHUNKS)
    def _(i):
        arrange_x(i)
        send_x(i)
        arrange_m(CHUNKS - 1 - i)
        send_m(CHUNKS - 1 - i)

    @pl.loop(1, ZERO)
    def _(d):
        to_peer(filt_ref.at[0], taps.at[behind(d)], f_snd, f_rcv, d).wait_recv()

    def forward_tile(t, with_lag):
        conv, sums = [], []
        rows = taps[t]
        for g in range(0, 8, 2):
            n = t * 8 + g
            wins = [windows(x_prev[n + e], x_own[n + e]) for e in range(2)]
            conv += pair_convolved([forward_taps(rows[g + e : g + e + 1]) for e in range(2)], wins)
            if with_lag:
                sums += [diagonal(v, True) for v in pair_lags([m_own[n], m_own[n + 1]], wins)]
        if with_lag:
            grads[t] = jnp.sum(jnp.stack(sums), axis=1)
        out = exchange(conv)
        for a in range(8):
            at = (slice(16 * a, 16 * a + 16), tile_of(t))
            qg[at] = (ct_in[at].astype(F32) * out[a].astype(F32)).astype(BF)

    def backward_tile(t, with_lag):
        conv, sums = [], []
        rows = taps[t]
        for g in range(0, 8, 2):
            n = t * 8 + g
            wins = [windows(m_own[n + e], m_next[n + e]) for e in range(2)]
            conv += pair_convolved([backward_taps(rows[g + e : g + e + 1]) for e in range(2)], wins)
            if with_lag:
                sums += [diagonal(v, False) for v in pair_lags([x_own[n], x_own[n + 1]], wins)]
        if with_lag:
            grads[t] = jnp.sum(jnp.stack(sums), axis=1)
        out = exchange(conv)
        for a in range(8):
            ig[16 * a : 16 * a + 16, tile_of(t)] = out[a]

    def store(vmem, hbm, sem, i):
        return pltpu.make_async_copy(vmem.at[:, wide(i)], hbm.at[0, :, wide(i)], sem.at[i])

    def stage(i, with_lag):
        j = CHUNKS - 1 - i

        @pl.when(has_prev)
        def _():
            x_copy(i).wait_recv()

        @pl.when(has_next)
        def _():
            m_copy(j).wait_recv()

        @pl.loop(0, TILES)
        def _(u):
            forward_tile(i * TILES + u, with_lag)
            backward_tile(j * TILES + u, with_lag)

        store(qg, qg_hbm, qg_st, i).start()
        store(ig, ig_hbm, ig_st, j).start()

    @pl.loop(0, HALF)
    def _(i):
        stage(i, True)

    @pl.loop(1, ZERO)
    def _(d):
        to_peer(grads.at[ahead(d)], shares.at[d], g_snd, g_rcv, d).start()

    @pl.loop(HALF, HALF + 2)
    def _(i):
        stage(i, False)

    @pl.loop(1, ZERO)
    def _(d):
        to_peer(grads.at[ahead(d)], shares.at[d], g_snd, g_rcv, d).wait_recv()

    shares[0] = grads[me]
    grad = jnp.sum(shares[...], axis=0)
    squares[0] = grad * grad

    @pl.loop(1, ZERO)
    def _(d):
        to_peer(squares.at[0], squares.at[d], s_snd, s_rcv, d).start()

    stage(HALF + 2, False)

    @pl.loop(1, ZERO)
    def _(d):
        to_peer(squares.at[0], squares.at[d], s_snd, s_rcv, d).wait_recv()

    total = jnp.sum(jnp.sum(squares[...], axis=0), axis=(0, 1), keepdims=True)
    norm = jnp.sqrt(jnp.broadcast_to(total, (8, 128)))
    clipped = grad * jnp.minimum(1.0, CLIP_NORM / (norm + 1e-06))
    count = jnp.full((8, 128), step_ref[0], jnp.int32).astype(F32) + 1.0
    moment_one = BETA_ONE * one_ref[0] + (1.0 - BETA_ONE) * clipped
    moment_two = BETA_TWO * two_ref[0] + (1.0 - BETA_TWO) * clipped * clipped
    corrected_one = moment_one / (1.0 - jnp.exp(count * math.log(BETA_ONE)))
    corrected_two = moment_two / (1.0 - jnp.exp(count * math.log(BETA_TWO)))
    stepped[...] = filt_ref[0] - LEARN_RATE * corrected_one / (jnp.sqrt(corrected_two) + ADAM_EPS)

    def to_mate(b):
        return pltpu.make_async_remote_copy(
            src_ref=stepped,
            dst_ref=partners.at[b],
            send_sem=p_snd.at[b],
            recv_sem=p_rcv.at[b],
            device_id={"rep": mates[b]},
            device_id_type=MESH,
        )

    for b in range(3):
        to_mate(b).start()

    stage(HALF + 3, False)

    for b in range(3):
        to_mate(b).wait_recv()
    bit = lax.rem(jnp.full((8, 128), step_ref[0], jnp.int32), 3)
    partner = jnp.where(bit == 0, partners[0], jnp.where(bit == 1, partners[1], partners[2]))
    new_ref[0] = 0.5 * (stepped[...] + partner)

    for b in range(3):
        to_mate(b).wait_send()

    @pl.loop(1, ZERO)
    def _(d):
        to_peer(filt_ref.at[0], taps.at[me], f_snd, f_rcv, d).wait_send()
        to_peer(grads.at[ahead(d)], shares.at[d], g_snd, g_rcv, d).wait_send()
        to_peer(squares.at[0], squares.at[d], s_snd, s_rcv, d).wait_send()

    @pl.loop(0, CHUNKS)
    def _(i):
        store(qg, qg_hbm, qg_st, i).wait()
        store(ig, ig_hbm, ig_st, i).wait()

        @pl.when(has_next)
        def _():
            x_copy(i).wait_send()

        @pl.when(has_prev)
        def _():
            m_copy(i).wait_send()


def on_device(gated_input, query_gate, cotangent, filters, first_moment, second_moment, step_index):
    anywhere = pl.BlockSpec(memory_space=pl.ANY)
    vmem = pl.BlockSpec(memory_space=pltpu.VMEM)
    dma = pltpu.SemaphoreType.DMA
    _, rows, channels = gated_input.shape
    groups = channels // 16
    natural = pltpu.VMEM((rows, channels), BF)
    grouped = pltpu.VMEM((groups, 16, 128), BF)
    shards = pltpu.VMEM((ZERO, 8, 128), F32)
    return pl.pallas_call(
        kernel,
        name="hyena_step",
        out_shape=[
            jax.ShapeDtypeStruct(gated_input.shape, BF),
            jax.ShapeDtypeStruct(gated_input.shape, BF),
            jax.ShapeDtypeStruct(filters.shape, F32),
        ],
        in_specs=[anywhere] * 3 + [vmem] * 3 + [pl.BlockSpec(memory_space=pltpu.SMEM)],
        out_specs=[anywhere] * 2 + [vmem],
        scratch_shapes=[natural] * 3
        + [grouped] * 4
        + [shards] * 4
        + [pltpu.VMEM((8, 128), F32), pltpu.VMEM((3, 8, 128), F32)]
        + [natural] * 2
        + [dma((CHUNKS,))] * 7
        + [dma((ZERO,))] * 6
        + [dma((3,))] * 2
        + [dma((CHUNKS,))] * 2,
        compiler_params=pltpu.CompilerParams(
            collective_id=0, has_side_effects=True, vmem_limit_bytes=40 << 20
        ),
        cost_estimate=pl.CostEstimate(flops=4 << 30, bytes_accessed=8 << 20, transcendentals=0),
    )(gated_input, query_gate, cotangent, filters, first_moment, second_moment, step_index)


def solution(mesh):
    split = P("rep", "zero", None)
    return jax.shard_map(
        on_device,
        mesh=mesh,
        in_specs=(split,) * 6 + (P(),),
        out_specs=(split,) * 3,
        check_vma=False,
    )
```

```python
import math

import jax
import jax.numpy as jnp
from jax import lax
from jax.experimental import pallas as pl
from jax.experimental.pallas import tpu as pltpu
from jax.sharding import PartitionSpec as P

CLIP_NORM = 1.0
BETA_ONE = 0.9
BETA_TWO = 0.95
LEARN_RATE = 0.05
ADAM_EPS = 1e-08

BF = jnp.bfloat16
F32 = jnp.float32
MESH = pl.DeviceIdType.MESH

ZERO = 32
CHUNKS = 16
TILES = 2
HALF = CHUNKS // 2
WIDE = TILES * 128
GROUPS = TILES * 8
EARLY = 8
RS_BESIDE = 5
NORM_BESIDE = 11


def lane_ids():
    return lax.broadcasted_iota(jnp.int32, (16, 128), 1)


def row_ids():
    return lax.broadcasted_iota(jnp.int32, (16, 128), 0)


def exchange(blocks):
    part = lane_ids() // 16
    r = [blocks[0]] + [pltpu.roll(blocks[a], 16 * a, 1) for a in range(1, 8)]
    for s in (1, 2, 4):
        pick = (part & s) != 0
        r = [jnp.where(pick, r[(i + s) % 8], r[i]) for i in range(8)]
    return [r[0]] + [pltpu.roll(r[8 - g], 128 - 16 * g, 1) for g in range(1, 8)]


def windows(low, high):
    lanes = lane_ids()
    out = [low]
    for q in range(1, 8):
        out.append(pltpu.roll(jnp.where(lanes >= 16 * q, low, high), 128 - 16 * q, 1))
    return out + [high]


def forward_taps(row):
    taps = jnp.take_along_axis(
        jnp.broadcast_to(row, (16, 128)), (row_ids() - lane_ids()) & 127, axis=1
    )
    keep = lane_ids() > row_ids()
    none = jnp.zeros_like(taps)
    first, last = jnp.where(keep, taps, none), jnp.where(keep, none, taps)
    return jnp.concatenate([first, last[:, :16]], axis=1).astype(BF)


def backward_taps(row):
    taps = jnp.take_along_axis(
        jnp.broadcast_to(row, (16, 128)), (lane_ids() - row_ids()) & 127, axis=1
    )
    keep = lane_ids() >= row_ids()
    none = jnp.zeros_like(taps)
    first, last = jnp.where(keep, taps, none), jnp.where(keep, none, taps)
    return jnp.concatenate([first, last[:, :16]], axis=1).astype(BF)


def pair_convolved(taps_two, wins_two):
    taps = jnp.concatenate(taps_two, axis=0)
    wins = jnp.concatenate(
        [jnp.concatenate([u, v], axis=1) for u, v in zip(*wins_two)], axis=0
    )
    out = jnp.dot(taps, wins, preferred_element_type=F32)
    return [out[:16, :128].astype(BF), out[16:, 128:].astype(BF)]


def pair_lags(own_two, wins_two):
    none = jnp.zeros((16, 128), BF)
    rows = jnp.concatenate(
        [jnp.concatenate([own_two[0], none], 1), jnp.concatenate([none, own_two[1]], 1)], 0
    )
    wins = jnp.concatenate(
        [jnp.concatenate([u, v], axis=1) for u, v in zip(*wins_two)], axis=0
    )
    out = lax.dot_general(rows, wins, (((1,), (1,)), ((), ())), preferred_element_type=F32)
    return [out[:16], out[16:]]


def diagonal(lag, forward):
    tail = jnp.concatenate([lag[:, 128:144], jnp.zeros((16, 112), F32)], axis=1)
    if forward:
        keep, index = lane_ids() > row_ids(), (row_ids() - lane_ids()) & 127
    else:
        keep, index = lane_ids() >= row_ids(), (lane_ids() + row_ids()) & 127
    turned = jnp.take_along_axis(jnp.where(keep, lag[:, :128], tail), index, axis=1)
    return turned[:8] + turned[8:]


def kernel(
    x_hbm,
    gate_hbm,
    ct_hbm,
    filt_hbm,
    one_hbm,
    two_hbm,
    step_ref,
    qg_hbm,
    ig_hbm,
    new_hbm,
    x_in,
    gate_in,
    ct_in,
    x_own,
    m_own,
    x_prev,
    m_next,
    qg,
    ig,
    taps,
    grads,
    shares,
    squares,
    small,
    partners,
    x_ld,
    gate_ld,
    ct_ld,
    x_snd,
    x_rcv,
    m_snd,
    m_rcv,
    qg_st,
    ig_st,
    small_sem,
    p_snd,
    p_rcv,
    peer_sem,
):
    me = lax.axis_index("zero")
    rep = lax.axis_index("rep")
    has_next = me < ZERO - 1
    has_prev = me > 0
    mates = [
        rep + 1 - 2 * lax.rem(rep, 2),
        rep + 2 - 4 * lax.rem(lax.div(rep, 2), 2),
        lax.rem(rep + 4, 8),
    ]
    filt, one, two, stepped, sibling, renewed = (small.at[i] for i in range(6))
    core = lax.rem(me, 2)
    chip = lax.div(me, 2)

    def ahead(d):
        return lax.rem(me + d, ZERO)

    barrier = pltpu.get_barrier_semaphore()

    @pl.loop(1, ZERO)
    def _(d):
        pl.semaphore_signal(barrier, 1, device_id={"zero": ahead(d)}, device_id_type=MESH)

    for mate in mates:
        pl.semaphore_signal(barrier, 1, device_id={"rep": mate}, device_id_type=MESH)

    def wide(i):
        return pl.ds(pl.multiple_of(i * WIDE, WIDE), WIDE)

    def load(hbm, vmem, sem, i):
        return pltpu.make_async_copy(hbm.at[0, :, wide(i)], vmem.at[:, wide(i)], sem.at[i])

    def load_small(hbm, i):
        return pltpu.make_async_copy(hbm.at[0], small.at[i], small_sem.at[i])

    for i, hbm in enumerate((filt_hbm, one_hbm, two_hbm)):
        load_small(hbm, i).start()

    @pl.loop(0, CHUNKS)
    def _(i):
        load(x_hbm, x_in, x_ld, i).start()
        load(ct_hbm, ct_in, ct_ld, CHUNKS - 1 - i).start()
        load(gate_hbm, gate_in, gate_ld, CHUNKS - 1 - i).start()

    @pl.when(me == 0)
    def _():
        x_prev[...] = jnp.zeros_like(x_prev)

    @pl.when(me == ZERO - 1)
    def _():
        m_next[...] = jnp.zeros_like(m_next)

    def slab(i):
        return pl.ds(i * GROUPS, GROUPS)

    def x_copy(i):
        return pltpu.make_async_remote_copy(
            src_ref=x_own.at[slab(i)],
            dst_ref=x_prev.at[slab(i)],
            send_sem=x_snd.at[i],
            recv_sem=x_rcv.at[i],
            device_id={"zero": ahead(1)},
            device_id_type=MESH,
        )

    def m_copy(i):
        return pltpu.make_async_remote_copy(
            src_ref=m_own.at[slab(i)],
            dst_ref=m_next.at[slab(i)],
            send_sem=m_snd.at[i],
            recv_sem=m_rcv.at[i],
            device_id={"zero": ahead(ZERO - 1)},
            device_id_type=MESH,
        )

    def tile_of(t):
        return pl.ds(pl.multiple_of(t * 128, 128), 128)

    def arrange(i, j):
        load(x_hbm, x_in, x_ld, i).wait()
        load(ct_hbm, ct_in, ct_ld, j).wait()
        load(gate_hbm, gate_in, gate_ld, j).wait()
        for u in range(TILES):
            t = i * TILES + u
            out = exchange([x_in[16 * a : 16 * a + 16, tile_of(t)] for a in range(8)])
            for g in range(8):
                x_own[t * 8 + g] = out[g]
            t = j * TILES + u
            mixed = [
                (
                    ct_in[16 * a : 16 * a + 16, tile_of(t)].astype(F32)
                    * gate_in[16 * a : 16 * a + 16, tile_of(t)].astype(F32)
                ).astype(BF)
                for a in range(8)
            ]
            out = exchange(mixed)
            for g in range(8):
                m_own[t * 8 + g] = out[g]

    def send_halo(i, j):
        @pl.when(has_next)
        def _():
            x_copy(i).start()

        @pl.when(has_prev)
        def _():
            m_copy(j).start()

    def wait_halo(i, j):
        @pl.when(has_prev)
        def _():
            x_copy(i).wait_recv()

        @pl.when(has_next)
        def _():
            m_copy(j).wait_recv()

    def to_peer(src, dst, kind, peer):
        return pltpu.make_async_remote_copy(
            src_ref=src,
            dst_ref=dst,
            send_sem=peer_sem.at[kind],
            recv_sem=peer_sem.at[kind + 4],
            device_id={"zero": peer},
            device_id_type=MESH,
        )

    def all_shares():
        ref = shares.at[pl.ds(1, ZERO - 1)]
        return to_peer(ref, ref, 2, ahead(1))

    row = pl.ds(0, 1)

    def all_rows():
        ref = squares.at[pl.ds(1, ZERO - 1), row]
        return to_peer(ref, ref, 3, ahead(1))

    arrange(0, CHUNKS - 1)
    pl.semaphore_wait(barrier, ZERO - 1 + len(mates))
    send_halo(0, CHUNKS - 1)

    def to_sibling():
        return to_peer(filt, sibling, 0, me + 1 - 2 * core)

    def to_chip(d):
        return to_peer(taps.at[chip], taps.at[chip], 1, lax.rem(me + 2 * d, ZERO))

    def all_chips():
        ref = taps.at[pl.ds(1, ZERO // 2 - 1)]
        return to_peer(ref, ref, 1, ahead(2))

    for i, hbm in enumerate((filt_hbm, one_hbm, two_hbm)):
        load_small(hbm, i).wait()
    to_sibling().start()

    @pl.loop(1, HALF)
    def _(i):
        arrange(i, CHUNKS - 1 - i)
        send_halo(i, CHUNKS - 1 - i)

    to_sibling().wait_recv()
    own_taps, other_taps = filt[...], sibling[...]
    first_core = core == 0
    taps[chip] = jnp.concatenate(
        [
            jnp.where(first_core, own_taps, other_taps),
            jnp.where(first_core, other_taps, own_taps),
        ],
        axis=0,
    ).astype(BF)

    @pl.loop(1, ZERO // 2)
    def _(d):
        to_chip(d).start()

    @pl.loop(HALF, EARLY)
    def _(i):
        arrange(i, CHUNKS - 1 - i)
        send_halo(i, CHUNKS - 1 - i)

    @pl.loop(EARLY, CHUNKS)
    def _(i):
        arrange(i, CHUNKS - 1 - i)

    def x_windows(n):
        return windows(x_prev[n], x_own[n])

    def m_windows(n):
        return windows(m_own[n], m_next[n])

    def lag_tile(t, wins_of, own, forward):
        sums = []
        for g in range(0, 8, 2):
            n = t * 8 + g
            lags = pair_lags([own[n], own[n + 1]], [wins_of(n), wins_of(n + 1)])
            sums += [diagonal(v, forward) for v in lags]
        grads[t] = jnp.sum(jnp.stack(sums), axis=1)

    def send_share(t):
        @pl.when(t != me)
        def _():
            d = lax.rem(t - me + ZERO, ZERO)
            to_peer(grads.at[t], shares.at[d], 2, t).start()

    @pl.loop(0, HALF)
    def _(i):
        j = CHUNKS - 1 - i
        wait_halo(i, j)

        for u in range(TILES):
            lag_tile(i * TILES + u, x_windows, m_own, True)
            lag_tile(j * TILES + u, m_windows, x_own, False)

        for u in range(TILES):
            send_share(i * TILES + u)
            send_share(j * TILES + u)

    @pl.loop(EARLY, CHUNKS)
    def _(i):
        send_halo(i, CHUNKS - 1 - i)

    all_chips().wait_recv()

    def conv_tile(t, rows, wins_of, taps_of):
        conv = []
        for g in range(0, 8, 2):
            n = t * 8 + g
            conv += pair_convolved(
                [taps_of(rows[g + e : g + e + 1]) for e in range(2)], [wins_of(n), wins_of(n + 1)]
            )
        return exchange(conv)

    def store(vmem, hbm, sem, i):
        return pltpu.make_async_copy(vmem.at[:, wide(i)], hbm.at[0, :, wide(i)], sem.at[i])

    def convolve(i):
        j = CHUNKS - 1 - i
        x_taps, m_taps = taps[i].astype(F32), taps[j].astype(F32)
        for u in range(TILES):
            t = i * TILES + u
            out = conv_tile(t, x_taps[8 * u : 8 * u + 8], x_windows, forward_taps)
            for a in range(8):
                at = (slice(16 * a, 16 * a + 16), tile_of(t))
                qg[at] = (ct_in[at].astype(F32) * out[a].astype(F32)).astype(BF)
            t = j * TILES + u
            out = conv_tile(t, m_taps[8 * u : 8 * u + 8], m_windows, backward_taps)
            for a in range(8):
                ig[16 * a : 16 * a + 16, tile_of(t)] = out[a]
        store(qg, qg_hbm, qg_st, i).start()
        store(ig, ig_hbm, ig_st, j).start()

    def convolve_late(i):
        wait_halo(i, CHUNKS - 1 - i)
        convolve(i)

    @pl.loop(0, RS_BESIDE)
    def _(i):
        convolve(i)

    count = jnp.full((8, 128), step_ref[0], jnp.int32).astype(F32) + 1.0
    rate = LEARN_RATE / (1.0 - jnp.exp(count * math.log(BETA_ONE)))
    spread = 1.0 / (1.0 - jnp.exp(count * math.log(BETA_TWO)))
    all_shares().wait_recv()
    shares[0] = grads[me]
    grad = jnp.sum(shares[...], axis=0)
    squares[0] = jnp.broadcast_to(jnp.sum(grad * grad, axis=0, keepdims=True), (8, 128))

    @pl.loop(1, ZERO)
    def _(d):
        to_peer(squares.at[0, row], squares.at[d, row], 3, ahead(d)).start()

    @pl.loop(RS_BESIDE, HALF)
    def _(i):
        convolve(i)

    @pl.loop(HALF, NORM_BESIDE)
    def _(i):
        convolve_late(i)

    all_rows().wait_recv()
    total = jnp.sum(squares[:, 0, :], axis=(0, 1), keepdims=True)
    norm = jnp.sqrt(jnp.broadcast_to(total, (8, 128)))
    clipped = grad * jnp.minimum(1.0, CLIP_NORM / (norm + 1e-06))
    moment_one = BETA_ONE * one[...] + (1.0 - BETA_ONE) * clipped
    moment_two = BETA_TWO * two[...] + (1.0 - BETA_TWO) * clipped * clipped
    stepped[...] = filt[...] - rate * moment_one / (jnp.sqrt(moment_two * spread) + ADAM_EPS)

    def to_mate(b):
        return pltpu.make_async_remote_copy(
            src_ref=stepped,
            dst_ref=partners.at[b],
            send_sem=p_snd.at[b],
            recv_sem=p_rcv.at[b],
            device_id={"rep": mates[b]},
            device_id_type=MESH,
        )

    for b in range(3):
        to_mate(b).start()

    @pl.loop(NORM_BESIDE, CHUNKS)
    def _(i):
        convolve_late(i)

    for b in range(3):
        to_mate(b).wait_recv()
    bit = lax.rem(jnp.full((8, 128), step_ref[0], jnp.int32), 3)
    partner = jnp.where(bit == 0, partners[0], jnp.where(bit == 1, partners[1], partners[2]))
    renewed[...] = 0.5 * (stepped[...] + partner)
    result = pltpu.make_async_copy(renewed, new_hbm.at[0], small_sem.at[3])
    result.start()

    for b in range(3):
        to_mate(b).wait_send()
    to_sibling().wait_send()
    all_chips().wait_send()
    all_shares().wait_send()
    all_rows().wait_send()

    @pl.loop(0, CHUNKS)
    def _(i):
        store(qg, qg_hbm, qg_st, i).wait()
        store(ig, ig_hbm, ig_st, i).wait()

        @pl.when(has_next)
        def _():
            x_copy(i).wait_send()

        @pl.when(has_prev)
        def _():
            m_copy(i).wait_send()

    result.wait()


def on_device(gated_input, query_gate, cotangent, filters, first_moment, second_moment, step_index):
    anywhere = pl.BlockSpec(memory_space=pl.ANY)
    dma = pltpu.SemaphoreType.DMA
    _, rows, channels = gated_input.shape
    groups = channels // 16
    natural = pltpu.VMEM((rows, channels), BF)
    grouped = pltpu.VMEM((groups, 16, 128), BF)
    shards = pltpu.VMEM((ZERO, 8, 128), F32)
    return pl.pallas_call(
        kernel,
        name="hyena_step",
        out_shape=[
            jax.ShapeDtypeStruct(gated_input.shape, BF),
            jax.ShapeDtypeStruct(gated_input.shape, BF),
            jax.ShapeDtypeStruct(filters.shape, F32),
        ],
        in_specs=[anywhere] * 6 + [pl.BlockSpec(memory_space=pltpu.SMEM)],
        out_specs=[anywhere] * 3,
        scratch_shapes=[natural] * 3
        + [grouped] * 4
        + [natural] * 2
        + [pltpu.VMEM((ZERO // 2, 16, 128), BF)]
        + [shards] * 3
        + [pltpu.VMEM((6, 8, 128), F32), pltpu.VMEM((3, 8, 128), F32)]
        + [dma((CHUNKS,))] * 9
        + [dma((4,)), dma((3,)), dma((3,)), dma((8,))],
        compiler_params=pltpu.CompilerParams(
            collective_id=0, has_side_effects=True, vmem_limit_bytes=62 << 20
        ),
        cost_estimate=pl.CostEstimate(flops=4 << 30, bytes_accessed=8 << 20, transcendentals=0),
    )(gated_input, query_gate, cotangent, filters, first_moment, second_moment, step_index)


def solution(mesh):
    split = P("rep", "zero", None)
    return jax.shard_map(
        on_device,
        mesh=mesh,
        in_specs=(split,) * 6 + (P(),),
        out_specs=(split,) * 3,
        check_vma=False,
    )
```

```python
import math

import jax
import jax.numpy as jnp
from jax import lax
from jax.experimental import pallas as pl
from jax.experimental.pallas import tpu as pltpu
from jax.sharding import PartitionSpec as P

CLIP_NORM = 1.0
BETA_ONE = 0.9
BETA_TWO = 0.95
LEARN_RATE = 0.05
ADAM_EPS = 1e-08

BF = jnp.bfloat16
F32 = jnp.float32
MESH = pl.DeviceIdType.MESH

ZERO = 32
CHUNKS = 16
TILES = 2
HALF = CHUNKS // 2
WIDE = TILES * 128
GROUPS = TILES * 8
RS_BESIDE = 4


def lane_ids():
    return lax.broadcasted_iota(jnp.int32, (16, 128), 1)


def row_ids():
    return lax.broadcasted_iota(jnp.int32, (16, 128), 0)


def exchange(blocks):
    part = lane_ids() // 16
    r = [blocks[0]] + [pltpu.roll(blocks[a], 16 * a, 1) for a in range(1, 8)]
    for s in (1, 2, 4):
        pick = (part & s) != 0
        r = [jnp.where(pick, r[(i + s) % 8], r[i]) for i in range(8)]
    return [r[0]] + [pltpu.roll(r[8 - g], 128 - 16 * g, 1) for g in range(1, 8)]


def windows(low, high):
    lanes = lane_ids()
    out = [low]
    for q in range(1, 8):
        out.append(pltpu.roll(jnp.where(lanes >= 16 * q, low, high), 128 - 16 * q, 1))
    return out + [high]


def forward_taps(row):
    taps = jnp.take_along_axis(
        jnp.broadcast_to(row, (16, 128)), (row_ids() - lane_ids()) & 127, axis=1
    )
    keep = lane_ids() > row_ids()
    none = jnp.zeros_like(taps)
    first, last = jnp.where(keep, taps, none), jnp.where(keep, none, taps)
    return jnp.concatenate([first, last[:, :16]], axis=1).astype(BF)


def backward_taps(row):
    taps = jnp.take_along_axis(
        jnp.broadcast_to(row, (16, 128)), (lane_ids() - row_ids()) & 127, axis=1
    )
    keep = lane_ids() >= row_ids()
    none = jnp.zeros_like(taps)
    first, last = jnp.where(keep, taps, none), jnp.where(keep, none, taps)
    return jnp.concatenate([first, last[:, :16]], axis=1).astype(BF)


def pair_convolved(taps_two, wins_two):
    taps = jnp.concatenate(taps_two, axis=0)
    wins = jnp.concatenate(
        [jnp.concatenate([u, v], axis=1) for u, v in zip(*wins_two)], axis=0
    )
    out = jnp.dot(taps, wins, preferred_element_type=F32)
    return [out[:16, :128].astype(BF), out[16:, 128:].astype(BF)]


def pair_lags(own_two, wins_two):
    none = jnp.zeros((16, 128), BF)
    rows = jnp.concatenate(
        [jnp.concatenate([own_two[0], none], 1), jnp.concatenate([none, own_two[1]], 1)], 0
    )
    wins = jnp.concatenate(
        [jnp.concatenate([u, v], axis=1) for u, v in zip(*wins_two)], axis=0
    )
    out = lax.dot_general(rows, wins, (((1,), (1,)), ((), ())), preferred_element_type=F32)
    return [out[:16], out[16:]]


def diagonal(lag, forward):
    tail = jnp.concatenate([lag[:, 128:144], jnp.zeros((16, 112), F32)], axis=1)
    if forward:
        keep, index = lane_ids() > row_ids(), (row_ids() - lane_ids()) & 127
    else:
        keep, index = lane_ids() >= row_ids(), (lane_ids() + row_ids()) & 127
    turned = jnp.take_along_axis(jnp.where(keep, lag[:, :128], tail), index, axis=1)
    return turned[:8] + turned[8:]


def kernel(
    x_hbm,
    gate_hbm,
    ct_hbm,
    small_hbm,
    step_ref,
    conv_hbm,
    ig_hbm,
    new_hbm,
    x_in,
    gate_in,
    ct_in,
    x_own,
    m_own,
    x_prev,
    m_next,
    conv,
    ig,
    taps,
    grads,
    shares,
    near,
    far,
    small,
    mate_small,
    mate_grad,
    x_ld,
    gate_ld,
    ct_ld,
    x_snd,
    x_rcv,
    m_snd,
    m_rcv,
    conv_st,
    ig_st,
    small_sem,
    p_snd,
    p_rcv,
    far_sem,
    peer_sem,
):
    me = lax.axis_index("zero")
    rep = lax.axis_index("rep")
    has_next = me < ZERO - 1
    has_prev = me > 0
    mates = [
        rep + 1 - 2 * lax.rem(rep, 2),
        rep + 2 - 4 * lax.rem(lax.div(rep, 2), 2),
        lax.rem(rep + 4, 8),
    ]
    filt, one, two, own_grad, sibling, renewed = (small.at[i] for i in range(6))
    block, place = lax.div(me, 8), lax.rem(me, 8)
    core = lax.rem(me, 2)
    chip = lax.div(me, 2)

    def ahead(d):
        return lax.rem(me + d, ZERO)

    last = CHUNKS - 1
    rest = (CHUNKS - 1) * WIDE

    def load(hbm, vmem, sem, which, at, size):
        cols = pl.ds(at, size)
        return pltpu.make_async_copy(hbm.at[0, :, cols], vmem.at[:, cols], sem.at[which])

    def load_first():
        return [
            load(x_hbm, x_in, x_ld, 0, 0, WIDE),
            load(ct_hbm, ct_in, ct_ld, 0, rest, WIDE),
            load(gate_hbm, gate_in, gate_ld, 0, rest, WIDE),
        ]

    def load_rest():
        return [
            load(x_hbm, x_in, x_ld, 1, WIDE, rest),
            load(ct_hbm, ct_in, ct_ld, 1, 0, rest),
            load(gate_hbm, gate_in, gate_ld, 1, 0, rest),
        ]

    def load_small():
        return [pltpu.make_async_copy(small_hbm, small.at[pl.ds(0, 3)], small_sem.at[0])]

    for copy in load_first() + load_rest() + load_small():
        copy.start()

    barrier = pltpu.get_barrier_semaphore()

    @pl.loop(1, ZERO)
    def _(d):
        pl.semaphore_signal(barrier, 1, device_id={"zero": ahead(d)}, device_id_type=MESH)

    for mate in mates:
        for d in range(4):
            other = {"rep": mate, "zero": lax.rem(me + 8 * d, ZERO)}
            pl.semaphore_signal(barrier, 1, device_id=other, device_id_type=MESH)

    @pl.when(me == 0)
    def _():
        x_prev[...] = jnp.zeros_like(x_prev)

    @pl.when(me == ZERO - 1)
    def _():
        m_next[...] = jnp.zeros_like(m_next)

    def slab(i):
        return pl.ds(i * GROUPS, GROUPS)

    def x_copy(i):
        return pltpu.make_async_remote_copy(
            src_ref=x_own.at[slab(i)],
            dst_ref=x_prev.at[slab(i)],
            send_sem=x_snd.at[i],
            recv_sem=x_rcv.at[i],
            device_id={"zero": ahead(1)},
            device_id_type=MESH,
        )

    def m_copy(i):
        return pltpu.make_async_remote_copy(
            src_ref=m_own.at[slab(i)],
            dst_ref=m_next.at[slab(i)],
            send_sem=m_snd.at[i],
            recv_sem=m_rcv.at[i],
            device_id={"zero": ahead(ZERO - 1)},
            device_id_type=MESH,
        )

    def tile_of(t):
        return pl.ds(pl.multiple_of(t * 128, 128), 128)

    def arrange(i, j):
        for u in range(TILES):
            t = i * TILES + u
            out = exchange([x_in[16 * a : 16 * a + 16, tile_of(t)] for a in range(8)])
            for g in range(8):
                x_own[t * 8 + g] = out[g]
            t = j * TILES + u
            mixed = [
                (
                    ct_in[16 * a : 16 * a + 16, tile_of(t)].astype(F32)
                    * gate_in[16 * a : 16 * a + 16, tile_of(t)].astype(F32)
                ).astype(BF)
                for a in range(8)
            ]
            out = exchange(mixed)
            for g in range(8):
                m_own[t * 8 + g] = out[g]

    def send_halo(i, j):
        @pl.when(has_next)
        def _():
            x_copy(i).start()

        @pl.when(has_prev)
        def _():
            m_copy(j).start()

    def wait_halo(i, j):
        @pl.when(has_prev)
        def _():
            x_copy(i).wait_recv()

        @pl.when(has_next)
        def _():
            m_copy(j).wait_recv()

    def to_peer(src, dst, kind, peer):
        return pltpu.make_async_remote_copy(
            src_ref=src,
            dst_ref=dst,
            send_sem=peer_sem.at[kind],
            recv_sem=peer_sem.at[kind + 4],
            device_id={"zero": peer},
            device_id_type=MESH,
        )

    def all_shares():
        ref = shares.at[pl.ds(1, ZERO - 1)]
        return to_peer(ref, ref, 2, ahead(1))

    row = pl.ds(0, 1)

    def to_near(d):
        return to_peer(near.at[0, row], near.at[d, row], 3, block * 8 + lax.rem(place + d, 8))

    def all_near():
        ref = near.at[pl.ds(1, 7), row]
        return to_peer(ref, ref, 3, ahead(1))

    def to_far(slot, src, dst):
        other = {"zero": lax.rem(me + 8 * (slot % 4), ZERO)}
        if slot >= 4:
            other["rep"] = mates[slot // 4 - 1]
        return pltpu.make_async_remote_copy(
            src_ref=src,
            dst_ref=dst,
            send_sem=far_sem.at[0],
            recv_sem=far_sem.at[1],
            device_id=other,
            device_id_type=MESH,
        )

    def all_far():
        ref = far.at[pl.ds(1, 15), row]
        return to_far(1, ref, ref)

    def to_mate(b, src, dst, kind):
        return pltpu.make_async_remote_copy(
            src_ref=src,
            dst_ref=dst,
            send_sem=p_snd.at[3 * kind + b],
            recv_sem=p_rcv.at[3 * kind + b],
            device_id={"rep": mates[b]},
            device_id_type=MESH,
        )

    def params_to_mate(b):
        return to_mate(b, small.at[pl.ds(0, 3)], mate_small.at[b], 0)

    def grad_to_mate(b):
        return to_mate(b, own_grad, mate_grad.at[b], 1)

    for copy in load_first():
        copy.wait()
    arrange(0, last)
    pl.semaphore_wait(barrier, ZERO - 1 + 4 * len(mates))
    send_halo(0, last)

    def to_sibling():
        return to_peer(filt, sibling, 0, me + 1 - 2 * core)

    def to_chip(d):
        return to_peer(taps.at[chip], taps.at[chip], 1, lax.rem(me + 2 * d, ZERO))

    def all_chips():
        ref = taps.at[pl.ds(1, ZERO // 2 - 1)]
        return to_peer(ref, ref, 1, ahead(2))

    for copy in load_rest() + load_small():
        copy.wait()
    to_sibling().start()

    @pl.loop(1, HALF)
    def _(i):
        arrange(i, CHUNKS - 1 - i)
        send_halo(i, CHUNKS - 1 - i)

    to_sibling().wait_recv()
    own_taps, other_taps = filt[...], sibling[...]
    first_core = core == 0
    taps[chip] = jnp.concatenate(
        [
            jnp.where(first_core, own_taps, other_taps),
            jnp.where(first_core, other_taps, own_taps),
        ],
        axis=0,
    ).astype(BF)

    @pl.loop(1, ZERO // 2)
    def _(d):
        to_chip(d).start()

    for b in range(3):
        params_to_mate(b).start()

    @pl.loop(HALF, CHUNKS)
    def _(i):
        arrange(i, CHUNKS - 1 - i)

    def x_windows(n):
        return windows(x_prev[n], x_own[n])

    def m_windows(n):
        return windows(m_own[n], m_next[n])

    def lag_tile(t, wins_of, own, forward):
        sums = []
        for g in range(0, 8, 2):
            n = t * 8 + g
            lags = pair_lags([own[n], own[n + 1]], [wins_of(n), wins_of(n + 1)])
            sums += [diagonal(v, forward) for v in lags]
        grads[t] = jnp.sum(jnp.stack(sums), axis=1)

    def send_share(t):
        @pl.when(t != me)
        def _():
            d = lax.rem(t - me + ZERO, ZERO)
            to_peer(grads.at[t], shares.at[d], 2, t).start()

    @pl.loop(0, HALF)
    def _(i):
        j = CHUNKS - 1 - i
        wait_halo(i, j)

        for u in range(TILES):
            lag_tile(i * TILES + u, x_windows, m_own, True)
            lag_tile(j * TILES + u, m_windows, x_own, False)

        for u in range(TILES):
            send_share(i * TILES + u)
            send_share(j * TILES + u)

    all_chips().wait_recv()

    def conv_tile(t, rows, wins_of, taps_of):
        done = []
        for g in range(0, 8, 2):
            n = t * 8 + g
            done += pair_convolved(
                [taps_of(rows[g + e : g + e + 1]) for e in range(2)], [wins_of(n), wins_of(n + 1)]
            )
        return exchange(done)

    cuts = (0, RS_BESIDE, HALF, CHUNKS - 2, CHUNKS)

    def stores(part):
        low, high = cuts[part] * WIDE, cuts[part + 1] * WIDE
        x_cols = pl.ds(low, high - low)
        m_cols = pl.ds(CHUNKS * WIDE - high, high - low)
        return [
            pltpu.make_async_copy(conv.at[:, x_cols], conv_hbm.at[0, :, x_cols], conv_st.at[part]),
            pltpu.make_async_copy(ig.at[:, m_cols], ig_hbm.at[0, :, m_cols], ig_st.at[part]),
        ]

    def store(part):
        for copy in stores(part):
            copy.start()

    def convolve(i):
        j = CHUNKS - 1 - i
        x_taps, m_taps = taps[i].astype(F32), taps[j].astype(F32)
        for u in range(TILES):
            t = i * TILES + u
            out = conv_tile(t, x_taps[8 * u : 8 * u + 8], x_windows, forward_taps)
            for a in range(8):
                at = (slice(16 * a, 16 * a + 16), tile_of(t))
                conv[at] = out[a]
            t = j * TILES + u
            out = conv_tile(t, m_taps[8 * u : 8 * u + 8], m_windows, backward_taps)
            for a in range(8):
                ig[16 * a : 16 * a + 16, tile_of(t)] = out[a]

    def convolve_late(i):
        wait_halo(i, CHUNKS - 1 - i)
        convolve(i)

    @pl.loop(0, RS_BESIDE)
    def _(i):
        send_halo(HALF + i, last - HALF - i)
        convolve(i)

    store(0)
    count = jnp.full((8, 128), step_ref[0], jnp.int32).astype(F32) + 1.0
    rate = LEARN_RATE / (1.0 - jnp.exp(count * math.log(BETA_ONE)))
    spread = 1.0 / (1.0 - jnp.exp(count * math.log(BETA_TWO)))
    all_shares().wait_recv()
    shares[0] = grads[me]
    grad = jnp.sum(shares[...], axis=0)
    own_grad[...] = grad
    near[0] = jnp.broadcast_to(jnp.sum(grad * grad, axis=0, keepdims=True), (8, 128))
    for d in range(1, 8):
        to_near(d).start()
    for b in range(3):
        grad_to_mate(b).start()

    @pl.loop(RS_BESIDE, HALF)
    def _(i):
        send_halo(HALF + i, last - HALF - i)
        convolve(i)

    all_near().wait_recv()
    near_sum = jnp.sum(near[:, 0, :], axis=0, keepdims=True)
    far[0] = jnp.broadcast_to(near_sum, (8, 128))
    for slot in range(1, 16):
        to_far(slot, far.at[0, row], far.at[slot, row]).start()
    store(1)

    @pl.loop(HALF, CHUNKS - 2)
    def _(i):
        convolve_late(i)

    store(2)

    @pl.loop(CHUNKS - 2, CHUNKS)
    def _(i):
        convolve_late(i)

    store(3)
    to_sibling().wait_send()
    all_chips().wait_send()
    all_shares().wait_send()
    all_near().wait_send()

    @pl.loop(0, CHUNKS)
    def _(i):
        @pl.when(has_next)
        def _():
            x_copy(i).wait_send()

        @pl.when(has_prev)
        def _():
            m_copy(i).wait_send()

    for b in range(3):
        params_to_mate(b).wait()
        grad_to_mate(b).wait()
    bit = lax.rem(jnp.full((8, 128), step_ref[0], jnp.int32), 3)

    def picked(of):
        return jnp.where(bit == 0, of(0), jnp.where(bit == 1, of(1), of(2)))

    mate_values = [picked(lambda b: mate_small[b, i]) for i in range(3)]
    mate_values.append(picked(lambda b: mate_grad[b]))

    def stepped(values, squares):
        weights, first, second, gradient = values
        total = jnp.sum(squares, axis=(0, 1), keepdims=True)
        norm = jnp.sqrt(jnp.broadcast_to(total, (8, 128)))
        clipped = gradient * jnp.minimum(1.0, CLIP_NORM / (norm + 1e-06))
        moment_one = BETA_ONE * first + (1.0 - BETA_ONE) * clipped
        moment_two = BETA_TWO * second + (1.0 - BETA_TWO) * clipped * clipped
        return weights - rate * moment_one / (jnp.sqrt(moment_two * spread) + ADAM_EPS)

    all_far().wait()
    low, high = far[0:8, 0, :], far[8:16, 0, :]
    four = lax.broadcasted_iota(jnp.int32, (8, 128), 0) < 4
    none = jnp.zeros((8, 128), F32)
    own_squares = jnp.where(four, low, none)
    mate_squares = jnp.where(
        bit == 0,
        jnp.where(four, none, low),
        jnp.where((bit == 1) == four, high, none),
    )
    own = stepped([filt[...], one[...], two[...], grad], own_squares)
    renewed[...] = 0.5 * (own + stepped(mate_values, mate_squares))
    result = pltpu.make_async_copy(renewed, new_hbm.at[0], small_sem.at[1])
    result.start()
    for part in range(4):
        for copy in stores(part):
            copy.wait()
    result.wait()


def on_device(gated_input, query_gate, cotangent, filters, first_moment, second_moment, step_index):
    anywhere = pl.BlockSpec(memory_space=pl.ANY)
    dma = pltpu.SemaphoreType.DMA
    _, rows, channels = gated_input.shape
    groups = channels // 16
    natural = pltpu.VMEM((rows, channels), BF)
    grouped = pltpu.VMEM((groups, 16, 128), BF)
    shards = pltpu.VMEM((ZERO, 8, 128), F32)
    shard = jnp.concatenate([filters, first_moment, second_moment], axis=0)
    conv, input_grad, new_filters = pl.pallas_call(
        kernel,
        name="hyena_step",
        out_shape=[
            jax.ShapeDtypeStruct(gated_input.shape, BF),
            jax.ShapeDtypeStruct(gated_input.shape, BF),
            jax.ShapeDtypeStruct(filters.shape, F32),
        ],
        in_specs=[anywhere] * 4 + [pl.BlockSpec(memory_space=pltpu.SMEM)],
        out_specs=[anywhere] * 3,
        scratch_shapes=[natural] * 3
        + [grouped] * 4
        + [natural] * 2
        + [pltpu.VMEM((ZERO // 2, 16, 128), BF)]
        + [shards] * 2
        + [pltpu.VMEM((8, 8, 128), F32), pltpu.VMEM((16, 8, 128), F32)]
        + [pltpu.VMEM((6, 8, 128), F32), pltpu.VMEM((3, 3, 8, 128), F32)]
        + [pltpu.VMEM((3, 8, 128), F32)]
        + [dma((2,))] * 3
        + [dma((CHUNKS,))] * 4
        + [dma((4,))] * 2
        + [dma((2,)), dma((6,)), dma((6,)), dma((2,)), dma((8,))],
        compiler_params=pltpu.CompilerParams(
            collective_id=0, has_side_effects=True, vmem_limit_bytes=51 << 20
        ),
        cost_estimate=pl.CostEstimate(flops=4 << 30, bytes_accessed=8 << 20, transcendentals=0),
    )(gated_input, query_gate, cotangent, shard, step_index)
    query_grad = (cotangent.astype(F32) * conv.astype(F32)).astype(BF)
    return query_grad, input_grad, new_filters


def solution(mesh):
    split = P("rep", "zero", None)
    return jax.shard_map(
        on_device,
        mesh=mesh,
        in_specs=(split,) * 6 + (P(),),
        out_specs=(split,) * 3,
        check_vma=False,
    )
```

```python
import math

import jax
import jax.numpy as jnp
from jax import lax
from jax.experimental import pallas as pl
from jax.experimental.pallas import tpu as pltpu
from jax.sharding import PartitionSpec as P

CLIP_NORM = 1.0
BETA_ONE = 0.9
BETA_TWO = 0.95
LEARN_RATE = 0.05
ADAM_EPS = 1e-08

BF = jnp.bfloat16
F32 = jnp.float32
MESH = pl.DeviceIdType.MESH

ZERO = 32
CHUNKS = 16
TILES = 2
HALF = CHUNKS // 2
WIDE = TILES * 128
GROUPS = TILES * 8
RS_BESIDE = 4


def lane_ids():
    return lax.broadcasted_iota(jnp.int32, (16, 128), 1)


def row_ids():
    return lax.broadcasted_iota(jnp.int32, (16, 128), 0)


def exchange(blocks):
    part = lane_ids() // 16
    r = [blocks[0]] + [pltpu.roll(blocks[a], 16 * a, 1) for a in range(1, 8)]
    for s in (1, 2, 4):
        pick = (part & s) != 0
        r = [jnp.where(pick, r[(i + s) % 8], r[i]) for i in range(8)]
    return [r[0]] + [pltpu.roll(r[8 - g], 128 - 16 * g, 1) for g in range(1, 8)]


def windows(low, high):
    lanes = lane_ids()
    out = [low]
    for q in range(1, 8):
        out.append(pltpu.roll(jnp.where(lanes >= 16 * q, low, high), 128 - 16 * q, 1))
    return out + [high]


def forward_taps(row):
    taps = jnp.take_along_axis(
        jnp.broadcast_to(row, (16, 128)), (row_ids() - lane_ids()) & 127, axis=1
    )
    keep = lane_ids() > row_ids()
    none = jnp.zeros_like(taps)
    first, last = jnp.where(keep, taps, none), jnp.where(keep, none, taps)
    return jnp.concatenate([first, last[:, :16]], axis=1).astype(BF)


def backward_taps(row):
    taps = jnp.take_along_axis(
        jnp.broadcast_to(row, (16, 128)), (lane_ids() - row_ids()) & 127, axis=1
    )
    keep = lane_ids() >= row_ids()
    none = jnp.zeros_like(taps)
    first, last = jnp.where(keep, taps, none), jnp.where(keep, none, taps)
    return jnp.concatenate([first, last[:, :16]], axis=1).astype(BF)


def pair_convolved(taps_two, wins_two):
    taps = jnp.concatenate(taps_two, axis=0)
    wins = jnp.concatenate(
        [jnp.concatenate([u, v], axis=1) for u, v in zip(*wins_two)], axis=0
    )
    out = jnp.dot(taps, wins, preferred_element_type=F32)
    return [out[:16, :128].astype(BF), out[16:, 128:].astype(BF)]


def pair_lags(own_two, wins_two):
    none = jnp.zeros((16, 128), BF)
    rows = jnp.concatenate(
        [jnp.concatenate([own_two[0], none], 1), jnp.concatenate([none, own_two[1]], 1)], 0
    )
    wins = jnp.concatenate(
        [jnp.concatenate([u, v], axis=1) for u, v in zip(*wins_two)], axis=0
    )
    out = lax.dot_general(rows, wins, (((1,), (1,)), ((), ())), preferred_element_type=F32)
    return [out[:16], out[16:]]


def diagonal(lag, forward):
    tail = jnp.concatenate([lag[:, 128:144], jnp.zeros((16, 112), F32)], axis=1)
    if forward:
        keep, index = lane_ids() > row_ids(), (row_ids() - lane_ids()) & 127
    else:
        keep, index = lane_ids() >= row_ids(), (lane_ids() + row_ids()) & 127
    turned = jnp.take_along_axis(jnp.where(keep, lag[:, :128], tail), index, axis=1)
    return turned[:8] + turned[8:]


def kernel(
    x_hbm,
    gate_hbm,
    ct_hbm,
    small_hbm,
    step_ref,
    conv,
    ig,
    new_ref,
    x_in,
    gate_in,
    ct_in,
    x_own,
    m_own,
    x_prev,
    m_next,
    taps,
    grads,
    shares,
    near,
    far,
    small,
    mate_small,
    x_ld,
    gate_ld,
    ct_ld,
    x_snd,
    x_rcv,
    m_snd,
    m_rcv,
    small_sem,
    p_snd,
    p_rcv,
    far_sem,
    peer_sem,
):
    me = lax.axis_index("zero")
    rep = lax.axis_index("rep")
    has_next = me < ZERO - 1
    has_prev = me > 0
    mates = [
        rep + 1 - 2 * lax.rem(rep, 2),
        rep + 2 - 4 * lax.rem(lax.div(rep, 2), 2),
        lax.rem(rep + 4, 8),
    ]
    filt, one, two, own_grad, sibling = (small.at[i] for i in range(5))
    block, place = lax.div(me, 8), lax.rem(me, 8)
    core = lax.rem(me, 2)
    chip = lax.div(me, 2)

    def ahead(d):
        return lax.rem(me + d, ZERO)

    last = CHUNKS - 1
    rest = (CHUNKS - 1) * WIDE

    def load(hbm, vmem, sem, which, at, size):
        cols = pl.ds(at, size)
        return pltpu.make_async_copy(hbm.at[0, :, cols], vmem.at[:, cols], sem.at[which])

    def load_first():
        return [
            load(x_hbm, x_in, x_ld, 0, 0, WIDE),
            load(ct_hbm, ct_in, ct_ld, 0, rest, WIDE),
            load(gate_hbm, gate_in, gate_ld, 0, rest, WIDE),
        ]

    def load_rest():
        return [
            load(x_hbm, x_in, x_ld, 1, WIDE, rest),
            load(ct_hbm, ct_in, ct_ld, 1, 0, rest),
            load(gate_hbm, gate_in, gate_ld, 1, 0, rest),
        ]

    def load_small():
        return [pltpu.make_async_copy(small_hbm, small.at[pl.ds(0, 3)], small_sem.at[0])]

    for copy in load_first() + load_rest() + load_small():
        copy.start()

    barrier = pltpu.get_barrier_semaphore()

    @pl.loop(1, ZERO)
    def _(d):
        pl.semaphore_signal(barrier, 1, device_id={"zero": ahead(d)}, device_id_type=MESH)

    for mate in mates:
        for d in range(4):
            other = {"rep": mate, "zero": lax.rem(me + 8 * d, ZERO)}
            pl.semaphore_signal(barrier, 1, device_id=other, device_id_type=MESH)

    @pl.when(me == 0)
    def _():
        x_prev[...] = jnp.zeros_like(x_prev)

    @pl.when(me == ZERO - 1)
    def _():
        m_next[...] = jnp.zeros_like(m_next)

    def slab(i):
        return pl.ds(i * GROUPS, GROUPS)

    def x_copy(i):
        return pltpu.make_async_remote_copy(
            src_ref=x_own.at[slab(i)],
            dst_ref=x_prev.at[slab(i)],
            send_sem=x_snd.at[i],
            recv_sem=x_rcv.at[i],
            device_id={"zero": ahead(1)},
            device_id_type=MESH,
        )

    def m_copy(i):
        return pltpu.make_async_remote_copy(
            src_ref=m_own.at[slab(i)],
            dst_ref=m_next.at[slab(i)],
            send_sem=m_snd.at[i],
            recv_sem=m_rcv.at[i],
            device_id={"zero": ahead(ZERO - 1)},
            device_id_type=MESH,
        )

    def tile_of(t):
        return pl.ds(pl.multiple_of(t * 128, 128), 128)

    def arrange(i, j):
        for u in range(TILES):
            t = i * TILES + u
            out = exchange([x_in[16 * a : 16 * a + 16, tile_of(t)] for a in range(8)])
            for g in range(8):
                x_own[t * 8 + g] = out[g]
            t = j * TILES + u
            mixed = [
                (
                    ct_in[16 * a : 16 * a + 16, tile_of(t)].astype(F32)
                    * gate_in[16 * a : 16 * a + 16, tile_of(t)].astype(F32)
                ).astype(BF)
                for a in range(8)
            ]
            out = exchange(mixed)
            for g in range(8):
                m_own[t * 8 + g] = out[g]

    def send_halo(i, j):
        @pl.when(has_next)
        def _():
            x_copy(i).start()

        @pl.when(has_prev)
        def _():
            m_copy(j).start()

    def wait_halo(i, j):
        @pl.when(has_prev)
        def _():
            x_copy(i).wait_recv()

        @pl.when(has_next)
        def _():
            m_copy(j).wait_recv()

    def to_peer(src, dst, kind, peer):
        return pltpu.make_async_remote_copy(
            src_ref=src,
            dst_ref=dst,
            send_sem=peer_sem.at[kind],
            recv_sem=peer_sem.at[kind + 4],
            device_id={"zero": peer},
            device_id_type=MESH,
        )

    def all_shares():
        ref = shares.at[pl.ds(1, ZERO - 1)]
        return to_peer(ref, ref, 2, ahead(1))

    row = pl.ds(0, 1)

    def to_near(d):
        return to_peer(near.at[0, row], near.at[d, row], 3, block * 8 + lax.rem(place + d, 8))

    def all_near():
        ref = near.at[pl.ds(1, 7), row]
        return to_peer(ref, ref, 3, ahead(1))

    def to_far(slot, src, dst):
        other = {"zero": lax.rem(me + 8 * (slot % 4), ZERO)}
        if slot >= 4:
            other["rep"] = mates[slot // 4 - 1]
        return pltpu.make_async_remote_copy(
            src_ref=src,
            dst_ref=dst,
            send_sem=far_sem.at[0],
            recv_sem=far_sem.at[1],
            device_id=other,
            device_id_type=MESH,
        )

    def all_far():
        ref = far.at[pl.ds(1, 15), row]
        return to_far(1, ref, ref)

    def to_mate(b):
        return pltpu.make_async_remote_copy(
            src_ref=small.at[pl.ds(0, 4)],
            dst_ref=mate_small.at[b],
            send_sem=p_snd.at[b],
            recv_sem=p_rcv.at[b],
            device_id={"rep": mates[b]},
            device_id_type=MESH,
        )

    for copy in load_first():
        copy.wait()
    arrange(0, last)
    pl.semaphore_wait(barrier, ZERO - 1 + 4 * len(mates))
    send_halo(0, last)

    def to_sibling():
        return to_peer(filt, sibling, 0, me + 1 - 2 * core)

    def to_chip(d):
        return to_peer(taps.at[chip], taps.at[chip], 1, lax.rem(me + 2 * d, ZERO))

    def all_chips():
        ref = taps.at[pl.ds(1, ZERO // 2 - 1)]
        return to_peer(ref, ref, 1, ahead(2))

    for copy in load_rest() + load_small():
        copy.wait()
    to_sibling().start()

    @pl.loop(1, HALF)
    def _(i):
        arrange(i, CHUNKS - 1 - i)
        send_halo(i, CHUNKS - 1 - i)

    to_sibling().wait_recv()
    own_taps, other_taps = filt[...], sibling[...]
    first_core = core == 0
    taps[chip] = jnp.concatenate(
        [
            jnp.where(first_core, own_taps, other_taps),
            jnp.where(first_core, other_taps, own_taps),
        ],
        axis=0,
    ).astype(BF)

    @pl.loop(1, ZERO // 2)
    def _(d):
        to_chip(d).start()

    @pl.loop(HALF, CHUNKS)
    def _(i):
        arrange(i, CHUNKS - 1 - i)

    def x_windows(n):
        return windows(x_prev[n], x_own[n])

    def m_windows(n):
        return windows(m_own[n], m_next[n])

    def lag_tile(t, wins_of, own, forward):
        sums = []
        for g in range(0, 8, 2):
            n = t * 8 + g
            lags = pair_lags([own[n], own[n + 1]], [wins_of(n), wins_of(n + 1)])
            sums += [diagonal(v, forward) for v in lags]
        grads[t] = jnp.sum(jnp.stack(sums), axis=1)

    def send_share(t):
        @pl.when(t != me)
        def _():
            d = lax.rem(t - me + ZERO, ZERO)
            to_peer(grads.at[t], shares.at[d], 2, t).start()

    @pl.loop(0, HALF)
    def _(i):
        j = CHUNKS - 1 - i
        wait_halo(i, j)

        for u in range(TILES):
            lag_tile(i * TILES + u, x_windows, m_own, True)
            lag_tile(j * TILES + u, m_windows, x_own, False)

        for u in range(TILES):
            send_share(i * TILES + u)
            send_share(j * TILES + u)

    all_chips().wait_recv()

    def conv_tile(t, rows, wins_of, taps_of):
        done = []
        for g in range(0, 8, 2):
            n = t * 8 + g
            done += pair_convolved(
                [taps_of(rows[g + e : g + e + 1]) for e in range(2)], [wins_of(n), wins_of(n + 1)]
            )
        return exchange(done)

    def convolve(i):
        j = CHUNKS - 1 - i
        x_taps, m_taps = taps[i].astype(F32), taps[j].astype(F32)
        for u in range(TILES):
            t = i * TILES + u
            out = conv_tile(t, x_taps[8 * u : 8 * u + 8], x_windows, forward_taps)
            for a in range(8):
                at = (slice(16 * a, 16 * a + 16), tile_of(t))
                conv[0, *at] = out[a]
            t = j * TILES + u
            out = conv_tile(t, m_taps[8 * u : 8 * u + 8], m_windows, backward_taps)
            for a in range(8):
                ig[0, 16 * a : 16 * a + 16, tile_of(t)] = out[a]

    def convolve_late(i):
        wait_halo(i, CHUNKS - 1 - i)
        convolve(i)

    @pl.loop(0, RS_BESIDE)
    def _(i):
        send_halo(HALF + i, last - HALF - i)
        convolve(i)

    count = jnp.full((8, 128), step_ref[0], jnp.int32).astype(F32) + 1.0
    rate = LEARN_RATE / (1.0 - jnp.exp(count * math.log(BETA_ONE)))
    spread = 1.0 / (1.0 - jnp.exp(count * math.log(BETA_TWO)))
    all_shares().wait_recv()
    shares[0] = grads[me]
    grad = jnp.sum(shares[...], axis=0)
    own_grad[...] = grad
    near[0] = jnp.broadcast_to(jnp.sum(grad * grad, axis=0, keepdims=True), (8, 128))
    for d in range(1, 8):
        to_near(d).start()
    for b in range(3):
        to_mate(b).start()

    @pl.loop(RS_BESIDE, HALF)
    def _(i):
        send_halo(HALF + i, last - HALF - i)
        convolve(i)

    all_near().wait_recv()
    near_sum = jnp.sum(near[:, 0, :], axis=0, keepdims=True)
    far[0] = jnp.broadcast_to(near_sum, (8, 128))
    for slot in range(1, 16):
        to_far(slot, far.at[0, row], far.at[slot, row]).start()
    @pl.loop(HALF, CHUNKS - 2)
    def _(i):
        convolve_late(i)

    @pl.loop(CHUNKS - 2, CHUNKS)
    def _(i):
        convolve_late(i)

    to_sibling().wait_send()
    all_chips().wait_send()
    all_shares().wait_send()
    all_near().wait_send()

    @pl.loop(0, CHUNKS)
    def _(i):
        @pl.when(has_next)
        def _():
            x_copy(i).wait_send()

        @pl.when(has_prev)
        def _():
            m_copy(i).wait_send()

    for b in range(3):
        to_mate(b).wait()
    bit = lax.rem(jnp.full((8, 128), step_ref[0], jnp.int32), 3)

    def picked(of):
        return jnp.where(bit == 0, of(0), jnp.where(bit == 1, of(1), of(2)))

    mate_values = [picked(lambda b: mate_small[b, i]) for i in range(4)]

    def stepped(values, squares):
        weights, first, second, gradient = values
        total = jnp.sum(squares, axis=(0, 1), keepdims=True)
        norm = jnp.sqrt(jnp.broadcast_to(total, (8, 128)))
        clipped = gradient * jnp.minimum(1.0, CLIP_NORM / (norm + 1e-06))
        moment_one = BETA_ONE * first + (1.0 - BETA_ONE) * clipped
        moment_two = BETA_TWO * second + (1.0 - BETA_TWO) * clipped * clipped
        return weights - rate * moment_one / (jnp.sqrt(moment_two * spread) + ADAM_EPS)

    all_far().wait()
    low, high = far[0:8, 0, :], far[8:16, 0, :]
    four = lax.broadcasted_iota(jnp.int32, (8, 128), 0) < 4
    none = jnp.zeros((8, 128), F32)
    own_squares = jnp.where(four, low, none)
    mate_squares = jnp.where(
        bit == 0,
        jnp.where(four, none, low),
        jnp.where((bit == 1) == four, high, none),
    )
    own = stepped([filt[...], one[...], two[...], grad], own_squares)
    new_ref[0] = 0.5 * (own + stepped(mate_values, mate_squares))


def on_device(gated_input, query_gate, cotangent, filters, first_moment, second_moment, step_index):
    anywhere = pl.BlockSpec(memory_space=pl.ANY)
    dma = pltpu.SemaphoreType.DMA
    _, rows, channels = gated_input.shape
    groups = channels // 16
    natural = pltpu.VMEM((rows, channels), BF)
    grouped = pltpu.VMEM((groups, 16, 128), BF)
    shards = pltpu.VMEM((ZERO, 8, 128), F32)
    shard = jnp.concatenate([filters, first_moment, second_moment], axis=0)
    conv, input_grad, new_filters = pl.pallas_call(
        kernel,
        name="hyena_step",
        out_shape=[
            jax.ShapeDtypeStruct(gated_input.shape, BF),
            jax.ShapeDtypeStruct(gated_input.shape, BF),
            jax.ShapeDtypeStruct(filters.shape, F32),
        ],
        in_specs=[anywhere] * 4 + [pl.BlockSpec(memory_space=pltpu.SMEM)],
        out_specs=[pl.BlockSpec(memory_space=pltpu.VMEM)] * 3,
        scratch_shapes=[natural] * 3
        + [grouped] * 4
        + [pltpu.VMEM((ZERO // 2, 16, 128), BF)]
        + [shards] * 2
        + [pltpu.VMEM((8, 8, 128), F32), pltpu.VMEM((16, 8, 128), F32)]
        + [pltpu.VMEM((5, 8, 128), F32), pltpu.VMEM((3, 4, 8, 128), F32)]
        + [dma((2,))] * 3
        + [dma((CHUNKS,))] * 4
        + [dma((1,)), dma((3,)), dma((3,)), dma((2,)), dma((8,))],
        compiler_params=pltpu.CompilerParams(
            collective_id=0, has_side_effects=True, vmem_limit_bytes=51 << 20
        ),
        cost_estimate=pl.CostEstimate(flops=4 << 30, bytes_accessed=8 << 20, transcendentals=0),
    )(gated_input, query_gate, cotangent, shard, step_index)
    query_grad = (cotangent.astype(F32) * conv.astype(F32)).astype(BF)
    return query_grad, input_grad, new_filters


def solution(mesh):
    split = P("rep", "zero", None)
    return jax.shard_map(
        on_device,
        mesh=mesh,
        in_specs=(split,) * 6 + (P(),),
        out_specs=(split,) * 3,
        check_vma=False,
    )
```

```python
import math

import jax
import jax.numpy as jnp
from jax import lax
from jax.experimental import pallas as pl
from jax.experimental.pallas import tpu as pltpu
from jax.sharding import PartitionSpec as P

CLIP_NORM = 1.0
BETA_ONE = 0.9
BETA_TWO = 0.95
LEARN_RATE = 0.05
ADAM_EPS = 1e-08

BF = jnp.bfloat16
F32 = jnp.float32
MESH = pl.DeviceIdType.MESH

ZERO = 32
CHUNKS = 16
TILES = 2
HALF = CHUNKS // 2
WIDE = TILES * 128
GROUPS = TILES * 8
RS_BESIDE = 4


def lane_ids():
    return lax.broadcasted_iota(jnp.int32, (16, 128), 1)


def row_ids():
    return lax.broadcasted_iota(jnp.int32, (16, 128), 0)


def exchange(blocks):
    part = lane_ids() // 16
    r = [blocks[0]] + [pltpu.roll(blocks[a], 16 * a, 1) for a in range(1, 8)]
    for s in (1, 2, 4):
        pick = (part & s) != 0
        r = [jnp.where(pick, r[(i + s) % 8], r[i]) for i in range(8)]
    return [r[0]] + [pltpu.roll(r[8 - g], 128 - 16 * g, 1) for g in range(1, 8)]


def windows(low, high):
    lanes = lane_ids()
    out = [low]
    for q in range(1, 8):
        out.append(pltpu.roll(jnp.where(lanes >= 16 * q, low, high), 128 - 16 * q, 1))
    return out + [high]


def forward_taps(row):
    taps = jnp.take_along_axis(
        jnp.broadcast_to(row, (16, 128)), (row_ids() - lane_ids()) & 127, axis=1
    )
    keep = lane_ids() > row_ids()
    none = jnp.zeros_like(taps)
    first, last = jnp.where(keep, taps, none), jnp.where(keep, none, taps)
    return jnp.concatenate([first, last[:, :16]], axis=1).astype(BF)


def backward_taps(row):
    taps = jnp.take_along_axis(
        jnp.broadcast_to(row, (16, 128)), (lane_ids() - row_ids()) & 127, axis=1
    )
    keep = lane_ids() >= row_ids()
    none = jnp.zeros_like(taps)
    first, last = jnp.where(keep, taps, none), jnp.where(keep, none, taps)
    return jnp.concatenate([first, last[:, :16]], axis=1).astype(BF)


def pair_convolved(taps_two, wins_two):
    taps = jnp.concatenate(taps_two, axis=0)
    wins = jnp.concatenate(
        [jnp.concatenate([u, v], axis=1) for u, v in zip(*wins_two)], axis=0
    )
    out = jnp.dot(taps, wins, preferred_element_type=F32)
    return [out[:16, :128].astype(BF), out[16:, 128:].astype(BF)]


def pair_lags(own_two, wins_two):
    none = jnp.zeros((16, 128), BF)
    rows = jnp.concatenate(
        [jnp.concatenate([own_two[0], none], 1), jnp.concatenate([none, own_two[1]], 1)], 0
    )
    wins = jnp.concatenate(
        [jnp.concatenate([u, v], axis=1) for u, v in zip(*wins_two)], axis=0
    )
    out = lax.dot_general(rows, wins, (((1,), (1,)), ((), ())), preferred_element_type=F32)
    return [out[:16], out[16:]]


def diagonal(lag, forward):
    tail = jnp.concatenate([lag[:, 128:144], jnp.zeros((16, 112), F32)], axis=1)
    if forward:
        keep, index = lane_ids() > row_ids(), (row_ids() - lane_ids()) & 127
    else:
        keep, index = lane_ids() >= row_ids(), (lane_ids() + row_ids()) & 127
    turned = jnp.take_along_axis(jnp.where(keep, lag[:, :128], tail), index, axis=1)
    return turned[:8] + turned[8:]


def kernel(
    x_hbm,
    gate_hbm,
    ct_hbm,
    small_hbm,
    step_ref,
    conv,
    ig,
    new_ref,
    x_in,
    gate_in,
    ct_in,
    x_own,
    m_own,
    x_prev,
    m_next,
    taps,
    grads,
    shares,
    near,
    far,
    small,
    mate_small,
    x_ld,
    gate_ld,
    ct_ld,
    x_snd,
    x_rcv,
    m_snd,
    m_rcv,
    small_sem,
    p_snd,
    p_rcv,
    far_sem,
    peer_sem,
):
    me = lax.axis_index("zero")
    rep = lax.axis_index("rep")
    has_next = me < ZERO - 1
    has_prev = me > 0
    mates = [
        rep + 1 - 2 * lax.rem(rep, 2),
        rep + 2 - 4 * lax.rem(lax.div(rep, 2), 2),
        lax.rem(rep + 4, 8),
    ]
    filt, one, two, own_grad, sibling = (small.at[i] for i in range(5))
    block, place = lax.div(me, 8), lax.rem(me, 8)
    core = lax.rem(me, 2)
    chip = lax.div(me, 2)

    def ahead(d):
        return lax.rem(me + d, ZERO)

    last = CHUNKS - 1
    rest = (CHUNKS - 1) * WIDE

    def load(hbm, vmem, sem, which, at, size):
        cols = pl.ds(at, size)
        return pltpu.make_async_copy(hbm.at[0, :, cols], vmem.at[:, cols], sem.at[which])

    def load_first():
        return [
            load(x_hbm, x_in, x_ld, 0, 0, WIDE),
            load(ct_hbm, ct_in, ct_ld, 0, rest, WIDE),
            load(gate_hbm, gate_in, gate_ld, 0, rest, WIDE),
        ]

    def load_rest():
        return [
            load(x_hbm, x_in, x_ld, 1, WIDE, rest),
            load(ct_hbm, ct_in, ct_ld, 1, 0, rest),
            load(gate_hbm, gate_in, gate_ld, 1, 0, rest),
        ]

    def load_small():
        return [pltpu.make_async_copy(small_hbm, small.at[pl.ds(0, 3)], small_sem.at[0])]

    for copy in load_first() + load_rest() + load_small():
        copy.start()

    barrier = pltpu.get_barrier_semaphore()

    @pl.loop(1, ZERO)
    def _(d):
        pl.semaphore_signal(barrier, 1, device_id={"zero": ahead(d)}, device_id_type=MESH)

    for mate in mates:
        for d in range(4):
            other = {"rep": mate, "zero": lax.rem(me + 8 * d, ZERO)}
            pl.semaphore_signal(barrier, 1, device_id=other, device_id_type=MESH)

    @pl.when(me == 0)
    def _():
        x_prev[...] = jnp.zeros_like(x_prev)

    @pl.when(me == ZERO - 1)
    def _():
        m_next[...] = jnp.zeros_like(m_next)

    def slab(i):
        return pl.ds(i * GROUPS, GROUPS)

    def x_copy(i):
        return pltpu.make_async_remote_copy(
            src_ref=x_own.at[slab(i)],
            dst_ref=x_prev.at[slab(i)],
            send_sem=x_snd.at[i],
            recv_sem=x_rcv.at[i],
            device_id={"zero": ahead(1)},
            device_id_type=MESH,
        )

    def m_copy(i):
        return pltpu.make_async_remote_copy(
            src_ref=m_own.at[slab(i)],
            dst_ref=m_next.at[slab(i)],
            send_sem=m_snd.at[i],
            recv_sem=m_rcv.at[i],
            device_id={"zero": ahead(ZERO - 1)},
            device_id_type=MESH,
        )

    def tile_of(t):
        return pl.ds(pl.multiple_of(t * 128, 128), 128)

    def arrange(i, j):
        for u in range(TILES):
            t = i * TILES + u
            out = exchange([x_in[16 * a : 16 * a + 16, tile_of(t)] for a in range(8)])
            for g in range(8):
                x_own[t * 8 + g] = out[g]
            t = j * TILES + u
            mixed = [
                (
                    ct_in[16 * a : 16 * a + 16, tile_of(t)].astype(F32)
                    * gate_in[16 * a : 16 * a + 16, tile_of(t)].astype(F32)
                ).astype(BF)
                for a in range(8)
            ]
            out = exchange(mixed)
            for g in range(8):
                m_own[t * 8 + g] = out[g]

    def send_halo(i, j):
        @pl.when(has_next)
        def _():
            x_copy(i).start()

        @pl.when(has_prev)
        def _():
            m_copy(j).start()

    def wait_halo(i, j):
        @pl.when(has_prev)
        def _():
            x_copy(i).wait_recv()

        @pl.when(has_next)
        def _():
            m_copy(j).wait_recv()

    def to_peer(src, dst, kind, peer):
        return pltpu.make_async_remote_copy(
            src_ref=src,
            dst_ref=dst,
            send_sem=peer_sem.at[kind],
            recv_sem=peer_sem.at[kind + 4],
            device_id={"zero": peer},
            device_id_type=MESH,
        )

    def all_shares():
        ref = shares.at[pl.ds(1, ZERO - 1)]
        return to_peer(ref, ref, 2, ahead(1))

    row = pl.ds(0, 1)

    def to_near(d):
        return to_peer(near.at[0, row], near.at[d, row], 3, block * 8 + lax.rem(place + d, 8))

    def all_near():
        ref = near.at[pl.ds(1, 7), row]
        return to_peer(ref, ref, 3, ahead(1))

    def to_far(slot, src, dst):
        other = {"zero": lax.rem(me + 8 * (slot % 4), ZERO)}
        if slot >= 4:
            other["rep"] = mates[slot // 4 - 1]
        return pltpu.make_async_remote_copy(
            src_ref=src,
            dst_ref=dst,
            send_sem=far_sem.at[0],
            recv_sem=far_sem.at[1],
            device_id=other,
            device_id_type=MESH,
        )

    def all_far():
        ref = far.at[pl.ds(1, 15), row]
        return to_far(1, ref, ref)

    def to_mate(b):
        return pltpu.make_async_remote_copy(
            src_ref=small.at[pl.ds(0, 4)],
            dst_ref=mate_small.at[b],
            send_sem=p_snd.at[b],
            recv_sem=p_rcv.at[b],
            device_id={"rep": mates[b]},
            device_id_type=MESH,
        )

    for copy in load_first():
        copy.wait()
    arrange(0, last)
    pl.semaphore_wait(barrier, ZERO - 1 + 4 * len(mates))
    send_halo(0, last)

    def to_sibling():
        return to_peer(filt, sibling, 0, me + 1 - 2 * core)

    def to_chip(d):
        return to_peer(taps.at[chip], taps.at[chip], 1, lax.rem(me + 2 * d, ZERO))

    def all_chips():
        ref = taps.at[pl.ds(1, ZERO // 2 - 1)]
        return to_peer(ref, ref, 1, ahead(2))

    for copy in load_rest() + load_small():
        copy.wait()
    to_sibling().start()

    @pl.loop(1, HALF)
    def _(i):
        arrange(i, CHUNKS - 1 - i)
        send_halo(i, CHUNKS - 1 - i)

    to_sibling().wait_recv()
    own_taps, other_taps = filt[...], sibling[...]
    first_core = core == 0
    taps[chip] = jnp.concatenate(
        [
            jnp.where(first_core, own_taps, other_taps),
            jnp.where(first_core, other_taps, own_taps),
        ],
        axis=0,
    ).astype(BF)

    @pl.loop(1, ZERO // 2)
    def _(d):
        to_chip(d).start()

    @pl.loop(HALF, CHUNKS)
    def _(i):
        arrange(i, CHUNKS - 1 - i)

    def x_windows(n):
        return windows(x_prev[n], x_own[n])

    def m_windows(n):
        return windows(m_own[n], m_next[n])

    def lag_tile(t, wins_of, own, forward):
        sums = []
        for g in range(0, 8, 2):
            n = t * 8 + g
            lags = pair_lags([own[n], own[n + 1]], [wins_of(n), wins_of(n + 1)])
            sums += [diagonal(v, forward) for v in lags]
        grads[t] = jnp.sum(jnp.stack(sums), axis=1)

    def send_share(t):
        @pl.when(t != me)
        def _():
            d = lax.rem(t - me + ZERO, ZERO)
            to_peer(grads.at[t], shares.at[d], 2, t).start()

    @pl.loop(0, HALF)
    def _(i):
        j = CHUNKS - 1 - i
        wait_halo(i, j)

        for u in range(TILES):
            lag_tile(i * TILES + u, x_windows, m_own, True)
            lag_tile(j * TILES + u, m_windows, x_own, False)

        for u in range(TILES):
            send_share(i * TILES + u)
            send_share(j * TILES + u)

    all_chips().wait_recv()

    def conv_tile(t, rows, wins_of, taps_of):
        done = []
        for g in range(0, 8, 2):
            n = t * 8 + g
            done += pair_convolved(
                [taps_of(rows[g + e : g + e + 1]) for e in range(2)], [wins_of(n), wins_of(n + 1)]
            )
        return exchange(done)

    def convolve(i):
        j = CHUNKS - 1 - i
        x_taps, m_taps = taps[i].astype(F32), taps[j].astype(F32)
        for u in range(TILES):
            t = i * TILES + u
            out = conv_tile(t, x_taps[8 * u : 8 * u + 8], x_windows, forward_taps)
            for a in range(8):
                at = (slice(16 * a, 16 * a + 16), tile_of(t))
                conv[0, *at] = (ct_in[at].astype(F32) * out[a].astype(F32)).astype(BF)
            t = j * TILES + u
            out = conv_tile(t, m_taps[8 * u : 8 * u + 8], m_windows, backward_taps)
            for a in range(8):
                ig[0, 16 * a : 16 * a + 16, tile_of(t)] = out[a]

    def convolve_late(i):
        wait_halo(i, CHUNKS - 1 - i)
        convolve(i)

    @pl.loop(0, RS_BESIDE)
    def _(i):
        send_halo(HALF + i, last - HALF - i)
        convolve(i)

    count = jnp.full((8, 128), step_ref[0], jnp.int32).astype(F32) + 1.0
    rate = LEARN_RATE / (1.0 - jnp.exp(count * math.log(BETA_ONE)))
    spread = 1.0 / (1.0 - jnp.exp(count * math.log(BETA_TWO)))
    all_shares().wait_recv()
    shares[0] = grads[me]
    grad = jnp.sum(shares[...], axis=0)
    own_grad[...] = grad
    near[0] = jnp.broadcast_to(jnp.sum(grad * grad, axis=0, keepdims=True), (8, 128))
    for d in range(1, 8):
        to_near(d).start()
    for b in range(3):
        to_mate(b).start()

    @pl.loop(RS_BESIDE, HALF)
    def _(i):
        send_halo(HALF + i, last - HALF - i)
        convolve(i)

    all_near().wait_recv()
    near_sum = jnp.sum(near[:, 0, :], axis=0, keepdims=True)
    far[0] = jnp.broadcast_to(near_sum, (8, 128))
    for slot in range(1, 16):
        to_far(slot, far.at[0, row], far.at[slot, row]).start()
    @pl.loop(HALF, CHUNKS - 2)
    def _(i):
        convolve_late(i)

    @pl.loop(CHUNKS - 2, CHUNKS)
    def _(i):
        convolve_late(i)

    to_sibling().wait_send()
    all_chips().wait_send()
    all_shares().wait_send()
    all_near().wait_send()

    @pl.loop(0, CHUNKS)
    def _(i):
        @pl.when(has_next)
        def _():
            x_copy(i).wait_send()

        @pl.when(has_prev)
        def _():
            m_copy(i).wait_send()

    for b in range(3):
        to_mate(b).wait()
    bit = lax.rem(jnp.full((8, 128), step_ref[0], jnp.int32), 3)

    def picked(of):
        return jnp.where(bit == 0, of(0), jnp.where(bit == 1, of(1), of(2)))

    mate_values = [picked(lambda b: mate_small[b, i]) for i in range(4)]

    def stepped(values, squares):
        weights, first, second, gradient = values
        total = jnp.sum(squares, axis=(0, 1), keepdims=True)
        norm = jnp.sqrt(jnp.broadcast_to(total, (8, 128)))
        clipped = gradient * jnp.minimum(1.0, CLIP_NORM / (norm + 1e-06))
        moment_one = BETA_ONE * first + (1.0 - BETA_ONE) * clipped
        moment_two = BETA_TWO * second + (1.0 - BETA_TWO) * clipped * clipped
        return weights - rate * moment_one / (jnp.sqrt(moment_two * spread) + ADAM_EPS)

    all_far().wait()
    low, high = far[0:8, 0, :], far[8:16, 0, :]
    four = lax.broadcasted_iota(jnp.int32, (8, 128), 0) < 4
    none = jnp.zeros((8, 128), F32)
    own_squares = jnp.where(four, low, none)
    mate_squares = jnp.where(
        bit == 0,
        jnp.where(four, none, low),
        jnp.where((bit == 1) == four, high, none),
    )
    own = stepped([filt[...], one[...], two[...], grad], own_squares)
    new_ref[0] = 0.5 * (own + stepped(mate_values, mate_squares))


def on_device(gated_input, query_gate, cotangent, filters, first_moment, second_moment, step_index):
    anywhere = pl.BlockSpec(memory_space=pl.ANY)
    dma = pltpu.SemaphoreType.DMA
    _, rows, channels = gated_input.shape
    groups = channels // 16
    natural = pltpu.VMEM((rows, channels), BF)
    grouped = pltpu.VMEM((groups, 16, 128), BF)
    shards = pltpu.VMEM((ZERO, 8, 128), F32)
    shard = jnp.concatenate([filters, first_moment, second_moment], axis=0)
    conv, input_grad, new_filters = pl.pallas_call(
        kernel,
        name="hyena_step",
        out_shape=[
            jax.ShapeDtypeStruct(gated_input.shape, BF),
            jax.ShapeDtypeStruct(gated_input.shape, BF),
            jax.ShapeDtypeStruct(filters.shape, F32),
        ],
        in_specs=[anywhere] * 4 + [pl.BlockSpec(memory_space=pltpu.SMEM)],
        out_specs=[pl.BlockSpec(memory_space=pltpu.VMEM)] * 3,
        scratch_shapes=[natural] * 3
        + [grouped] * 4
        + [pltpu.VMEM((ZERO // 2, 16, 128), BF)]
        + [shards] * 2
        + [pltpu.VMEM((8, 8, 128), F32), pltpu.VMEM((16, 8, 128), F32)]
        + [pltpu.VMEM((5, 8, 128), F32), pltpu.VMEM((3, 4, 8, 128), F32)]
        + [dma((2,))] * 3
        + [dma((CHUNKS,))] * 4
        + [dma((1,)), dma((3,)), dma((3,)), dma((2,)), dma((8,))],
        compiler_params=pltpu.CompilerParams(
            collective_id=0, has_side_effects=True, vmem_limit_bytes=51 << 20
        ),
        cost_estimate=pl.CostEstimate(flops=4 << 30, bytes_accessed=8 << 20, transcendentals=0),
    )(gated_input, query_gate, cotangent, shard, step_index)
    return conv, input_grad, new_filters


def solution(mesh):
    split = P("rep", "zero", None)
    return jax.shard_map(
        on_device,
        mesh=mesh,
        in_specs=(split,) * 6 + (P(),),
        out_specs=(split,) * 3,
        check_vma=False,
    )
```

```python
import math

import jax
import jax.numpy as jnp
from jax import lax
from jax.experimental import pallas as pl
from jax.experimental.pallas import tpu as pltpu
from jax.sharding import PartitionSpec as P

CLIP_NORM = 1.0
BETA_ONE = 0.9
BETA_TWO = 0.95
LEARN_RATE = 0.05
ADAM_EPS = 1e-08

BF = jnp.bfloat16
F32 = jnp.float32
MESH = pl.DeviceIdType.MESH

ZERO = 32
CHUNKS = 16
TILES = 2
HALF = CHUNKS // 2
WIDE = TILES * 128
GROUPS = TILES * 8
RS_BESIDE = 4


def lane_ids():
    return lax.broadcasted_iota(jnp.int32, (16, 128), 1)


def row_ids():
    return lax.broadcasted_iota(jnp.int32, (16, 128), 0)


def exchange(blocks):
    part = lane_ids() // 16
    r = [blocks[0]] + [pltpu.roll(blocks[a], 16 * a, 1) for a in range(1, 8)]
    for s in (1, 2, 4):
        pick = (part & s) != 0
        r = [jnp.where(pick, r[(i + s) % 8], r[i]) for i in range(8)]
    return [r[0]] + [pltpu.roll(r[8 - g], 128 - 16 * g, 1) for g in range(1, 8)]


def windows(low, high):
    lanes = lane_ids()
    out = [low]
    for q in range(1, 8):
        out.append(pltpu.roll(jnp.where(lanes >= 16 * q, low, high), 128 - 16 * q, 1))
    return out + [high]


def forward_taps(row):
    taps = jnp.take_along_axis(
        jnp.broadcast_to(row, (16, 128)), (row_ids() - lane_ids()) & 127, axis=1
    )
    keep = lane_ids() > row_ids()
    none = jnp.zeros_like(taps)
    first, last = jnp.where(keep, taps, none), jnp.where(keep, none, taps)
    return jnp.concatenate([first, last[:, :16]], axis=1).astype(BF)


def backward_taps(row):
    taps = jnp.take_along_axis(
        jnp.broadcast_to(row, (16, 128)), (lane_ids() - row_ids()) & 127, axis=1
    )
    keep = lane_ids() >= row_ids()
    none = jnp.zeros_like(taps)
    first, last = jnp.where(keep, taps, none), jnp.where(keep, none, taps)
    return jnp.concatenate([first, last[:, :16]], axis=1).astype(BF)


def pair_convolved(taps_two, wins_two):
    taps = jnp.concatenate(taps_two, axis=0)
    wins = jnp.concatenate(
        [jnp.concatenate([u, v], axis=1) for u, v in zip(*wins_two)], axis=0
    )
    out = jnp.dot(taps, wins, preferred_element_type=F32)
    return [out[:16, :128].astype(BF), out[16:, 128:].astype(BF)]


def pair_lags(own_two, wins_two):
    none = jnp.zeros((16, 128), BF)
    rows = jnp.concatenate(
        [jnp.concatenate([own_two[0], none], 1), jnp.concatenate([none, own_two[1]], 1)], 0
    )
    wins = jnp.concatenate(
        [jnp.concatenate([u, v], axis=1) for u, v in zip(*wins_two)], axis=0
    )
    out = lax.dot_general(rows, wins, (((1,), (1,)), ((), ())), preferred_element_type=F32)
    return [out[:16], out[16:]]


def diagonal(lag, forward):
    tail = jnp.concatenate([lag[:, 128:144], jnp.zeros((16, 112), F32)], axis=1)
    if forward:
        keep, index = lane_ids() > row_ids(), (row_ids() - lane_ids()) & 127
    else:
        keep, index = lane_ids() >= row_ids(), (lane_ids() + row_ids()) & 127
    turned = jnp.take_along_axis(jnp.where(keep, lag[:, :128], tail), index, axis=1)
    return turned[:8] + turned[8:]


def kernel(
    x_hbm,
    gate_hbm,
    ct_hbm,
    small_hbm,
    step_ref,
    conv,
    ig,
    new_ref,
    x_in,
    gate_in,
    ct_in,
    x_own,
    m_own,
    x_prev,
    m_next,
    taps,
    grads,
    shares,
    near,
    far,
    small,
    mate_small,
    x_ld,
    gate_ld,
    ct_ld,
    x_snd,
    x_rcv,
    m_snd,
    m_rcv,
    small_sem,
    p_snd,
    p_rcv,
    far_sem,
    peer_sem,
):
    me = lax.axis_index("zero")
    rep = lax.axis_index("rep")
    has_next = me < ZERO - 1
    has_prev = me > 0
    mates = [
        rep + 1 - 2 * lax.rem(rep, 2),
        rep + 2 - 4 * lax.rem(lax.div(rep, 2), 2),
        lax.rem(rep + 4, 8),
    ]
    filt, one, two, own_grad, sibling = (small.at[i] for i in range(5))
    block, place = lax.div(me, 8), lax.rem(me, 8)
    core = lax.rem(me, 2)
    chip = lax.div(me, 2)

    def ahead(d):
        return lax.rem(me + d, ZERO)

    last = CHUNKS - 1
    rest = (CHUNKS - 1) * WIDE

    def load(hbm, vmem, sem, which, at, size):
        cols = pl.ds(at, size)
        return pltpu.make_async_copy(hbm.at[0, :, cols], vmem.at[:, cols], sem.at[which])

    def load_first():
        return [
            load(x_hbm, x_in, x_ld, 0, 0, WIDE),
            load(ct_hbm, ct_in, ct_ld, 0, rest, WIDE),
            load(gate_hbm, gate_in, gate_ld, 0, rest, WIDE),
        ]

    def load_rest():
        return [
            load(x_hbm, x_in, x_ld, 1, WIDE, rest),
            load(ct_hbm, ct_in, ct_ld, 1, 0, rest),
            load(gate_hbm, gate_in, gate_ld, 1, 0, rest),
        ]

    def load_small():
        return [pltpu.make_async_copy(small_hbm, small.at[pl.ds(0, 3)], small_sem.at[0])]

    for copy in load_first() + load_rest() + load_small():
        copy.start()

    barrier = pltpu.get_barrier_semaphore()

    @pl.loop(1, ZERO)
    def _(d):
        pl.semaphore_signal(barrier, 1, device_id={"zero": ahead(d)}, device_id_type=MESH)

    for mate in mates:
        for d in range(4):
            other = {"rep": mate, "zero": lax.rem(me + 8 * d, ZERO)}
            pl.semaphore_signal(barrier, 1, device_id=other, device_id_type=MESH)

    @pl.when(me == 0)
    def _():
        x_prev[...] = jnp.zeros_like(x_prev)

    @pl.when(me == ZERO - 1)
    def _():
        m_next[...] = jnp.zeros_like(m_next)

    def slab(i):
        return pl.ds(i * GROUPS, GROUPS)

    def x_copy(i):
        return pltpu.make_async_remote_copy(
            src_ref=x_own.at[slab(i)],
            dst_ref=x_prev.at[slab(i)],
            send_sem=x_snd.at[i],
            recv_sem=x_rcv.at[i],
            device_id={"zero": ahead(1)},
            device_id_type=MESH,
        )

    def m_copy(i):
        return pltpu.make_async_remote_copy(
            src_ref=m_own.at[slab(i)],
            dst_ref=m_next.at[slab(i)],
            send_sem=m_snd.at[i],
            recv_sem=m_rcv.at[i],
            device_id={"zero": ahead(ZERO - 1)},
            device_id_type=MESH,
        )

    def tile_of(t):
        return pl.ds(pl.multiple_of(t * 128, 128), 128)

    def arrange(i, j):
        for u in range(TILES):
            t = i * TILES + u
            out = exchange([x_in[16 * a : 16 * a + 16, tile_of(t)] for a in range(8)])
            for g in range(8):
                x_own[t * 8 + g] = out[g]
            t = j * TILES + u
            mixed = [
                (
                    ct_in[16 * a : 16 * a + 16, tile_of(t)].astype(F32)
                    * gate_in[16 * a : 16 * a + 16, tile_of(t)].astype(F32)
                ).astype(BF)
                for a in range(8)
            ]
            out = exchange(mixed)
            for g in range(8):
                m_own[t * 8 + g] = out[g]

    def send_halo(i, j):
        @pl.when(has_next)
        def _():
            x_copy(i).start()

        @pl.when(has_prev)
        def _():
            m_copy(j).start()

    def wait_halo(i, j):
        @pl.when(has_prev)
        def _():
            x_copy(i).wait_recv()

        @pl.when(has_next)
        def _():
            m_copy(j).wait_recv()

    def to_peer(src, dst, kind, peer):
        return pltpu.make_async_remote_copy(
            src_ref=src,
            dst_ref=dst,
            send_sem=peer_sem.at[kind],
            recv_sem=peer_sem.at[kind + 4],
            device_id={"zero": peer},
            device_id_type=MESH,
        )

    def all_shares():
        ref = shares.at[pl.ds(1, ZERO - 1)]
        return to_peer(ref, ref, 2, ahead(1))

    row = pl.ds(0, 1)

    def to_near(d):
        return to_peer(near.at[0, row], near.at[d, row], 3, block * 8 + lax.rem(place + d, 8))

    def all_near():
        ref = near.at[pl.ds(1, 7), row]
        return to_peer(ref, ref, 3, ahead(1))

    def to_far(slot, src, dst):
        other = {"zero": lax.rem(me + 8 * (slot % 4), ZERO)}
        if slot >= 4:
            other["rep"] = mates[slot // 4 - 1]
        return pltpu.make_async_remote_copy(
            src_ref=src,
            dst_ref=dst,
            send_sem=far_sem.at[0],
            recv_sem=far_sem.at[1],
            device_id=other,
            device_id_type=MESH,
        )

    def all_far():
        ref = far.at[pl.ds(1, 15), row]
        return to_far(1, ref, ref)

    def to_mate(b):
        return pltpu.make_async_remote_copy(
            src_ref=small.at[pl.ds(0, 4)],
            dst_ref=mate_small.at[b],
            send_sem=p_snd.at[b],
            recv_sem=p_rcv.at[b],
            device_id={"rep": mates[b]},
            device_id_type=MESH,
        )

    for copy in load_first():
        copy.wait()
    arrange(0, last)
    pl.semaphore_wait(barrier, ZERO - 1 + 4 * len(mates))
    send_halo(0, last)

    def to_sibling():
        return to_peer(filt, sibling, 0, me + 1 - 2 * core)

    def to_chip(d):
        return to_peer(taps.at[chip], taps.at[chip], 1, lax.rem(me + 2 * d, ZERO))

    def all_chips():
        ref = taps.at[pl.ds(1, ZERO // 2 - 1)]
        return to_peer(ref, ref, 1, ahead(2))

    for copy in load_rest() + load_small():
        copy.wait()
    to_sibling().start()

    @pl.loop(1, HALF)
    def _(i):
        arrange(i, CHUNKS - 1 - i)
        send_halo(i, CHUNKS - 1 - i)

    to_sibling().wait_recv()
    own_taps, other_taps = filt[...], sibling[...]
    first_core = core == 0
    taps[chip] = jnp.concatenate(
        [
            jnp.where(first_core, own_taps, other_taps),
            jnp.where(first_core, other_taps, own_taps),
        ],
        axis=0,
    ).astype(BF)

    @pl.loop(1, ZERO // 2)
    def _(d):
        to_chip(d).start()

    @pl.loop(HALF, CHUNKS)
    def _(i):
        arrange(i, CHUNKS - 1 - i)

    def x_windows(n):
        return windows(x_prev[n], x_own[n])

    def m_windows(n):
        return windows(m_own[n], m_next[n])

    def lag_tile(t, wins_of, own, forward):
        sums = []
        for g in range(0, 8, 2):
            n = t * 8 + g
            lags = pair_lags([own[n], own[n + 1]], [wins_of(n), wins_of(n + 1)])
            sums += [diagonal(v, forward) for v in lags]
        grads[t] = jnp.sum(jnp.stack(sums), axis=1)

    def send_share(t):
        @pl.when(t != me)
        def _():
            d = lax.rem(t - me + ZERO, ZERO)
            to_peer(grads.at[t], shares.at[d], 2, t).start()

    @pl.loop(0, HALF)
    def _(i):
        j = CHUNKS - 1 - i
        wait_halo(i, j)

        for u in range(TILES):
            lag_tile(i * TILES + u, x_windows, m_own, True)
            lag_tile(j * TILES + u, m_windows, x_own, False)

        for u in range(TILES):
            send_share(i * TILES + u)
            send_share(j * TILES + u)

    all_chips().wait_recv()

    def conv_tile(t, rows, wins_of, taps_of):
        done = []
        for g in range(0, 8, 2):
            n = t * 8 + g
            done += pair_convolved(
                [taps_of(rows[g + e : g + e + 1]) for e in range(2)], [wins_of(n), wins_of(n + 1)]
            )
        return exchange(done)

    def convolve(i):
        j = CHUNKS - 1 - i
        x_taps, m_taps = taps[i].astype(F32), taps[j].astype(F32)
        for u in range(TILES):
            t = i * TILES + u
            out = conv_tile(t, x_taps[8 * u : 8 * u + 8], x_windows, forward_taps)
            for a in range(8):
                at = (slice(16 * a, 16 * a + 16), tile_of(t))
                conv[0, *at] = (ct_in[at].astype(F32) * out[a].astype(F32)).astype(BF)
            t = j * TILES + u
            out = conv_tile(t, m_taps[8 * u : 8 * u + 8], m_windows, backward_taps)
            for a in range(8):
                ig[0, 16 * a : 16 * a + 16, tile_of(t)] = out[a]

    def convolve_late(i):
        wait_halo(i, CHUNKS - 1 - i)
        convolve(i)

    @pl.loop(0, RS_BESIDE)
    def _(i):
        send_halo(HALF + i, last - HALF - i)
        convolve(i)

    count = jnp.full((8, 128), step_ref[0], jnp.int32).astype(F32) + 1.0
    rate = LEARN_RATE / (1.0 - jnp.exp(count * math.log(BETA_ONE)))
    spread = 1.0 / (1.0 - jnp.exp(count * math.log(BETA_TWO)))
    all_shares().wait_recv()
    shares[0] = grads[me]
    grad = jnp.sum(shares[...], axis=0)
    own_grad[...] = grad
    near[0] = jnp.broadcast_to(jnp.sum(grad * grad, axis=0, keepdims=True), (8, 128))
    for d in range(1, 8):
        to_near(d).start()
    for b in range(3):
        to_mate(b).start()

    @pl.loop(RS_BESIDE, HALF)
    def _(i):
        send_halo(HALF + i, last - HALF - i)
        convolve(i)

    all_near().wait_recv()
    near_sum = jnp.sum(near[:, 0, :], axis=0, keepdims=True)
    far[0] = jnp.broadcast_to(near_sum, (8, 128))
    for slot in reversed(range(1, 16)):
        to_far(slot, far.at[0, row], far.at[slot, row]).start()
    @pl.loop(HALF, CHUNKS - 2)
    def _(i):
        convolve_late(i)

    @pl.loop(CHUNKS - 2, CHUNKS)
    def _(i):
        convolve_late(i)

    to_sibling().wait_send()
    all_chips().wait_send()
    all_shares().wait_send()
    all_near().wait_send()

    @pl.loop(0, CHUNKS)
    def _(i):
        @pl.when(has_next)
        def _():
            x_copy(i).wait_send()

        @pl.when(has_prev)
        def _():
            m_copy(i).wait_send()

    for b in range(3):
        to_mate(b).wait()
    bit = lax.rem(jnp.full((8, 128), step_ref[0], jnp.int32), 3)

    def picked(of):
        return jnp.where(bit == 0, of(0), jnp.where(bit == 1, of(1), of(2)))

    mate_values = [picked(lambda b: mate_small[b, i]) for i in range(4)]

    def stepped(values, squares):
        weights, first, second, gradient = values
        total = jnp.sum(squares, axis=(0, 1), keepdims=True)
        norm = jnp.sqrt(jnp.broadcast_to(total, (8, 128)))
        clipped = gradient * jnp.minimum(1.0, CLIP_NORM / (norm + 1e-06))
        moment_one = BETA_ONE * first + (1.0 - BETA_ONE) * clipped
        moment_two = BETA_TWO * second + (1.0 - BETA_TWO) * clipped * clipped
        return weights - rate * moment_one / (jnp.sqrt(moment_two * spread) + ADAM_EPS)

    all_far().wait()
    low, high = far[0:8, 0, :], far[8:16, 0, :]
    four = lax.broadcasted_iota(jnp.int32, (8, 128), 0) < 4
    none = jnp.zeros((8, 128), F32)
    own_squares = jnp.where(four, low, none)
    mate_squares = jnp.where(
        bit == 0,
        jnp.where(four, none, low),
        jnp.where((bit == 1) == four, high, none),
    )
    own = stepped([filt[...], one[...], two[...], grad], own_squares)
    new_ref[0] = 0.5 * (own + stepped(mate_values, mate_squares))


def on_device(gated_input, query_gate, cotangent, filters, first_moment, second_moment, step_index):
    anywhere = pl.BlockSpec(memory_space=pl.ANY)
    dma = pltpu.SemaphoreType.DMA
    _, rows, channels = gated_input.shape
    groups = channels // 16
    natural = pltpu.VMEM((rows, channels), BF)
    grouped = pltpu.VMEM((groups, 16, 128), BF)
    shards = pltpu.VMEM((ZERO, 8, 128), F32)
    shard = jnp.concatenate([filters, first_moment, second_moment], axis=0)
    conv, input_grad, new_filters = pl.pallas_call(
        kernel,
        name="hyena_step",
        out_shape=[
            jax.ShapeDtypeStruct(gated_input.shape, BF),
            jax.ShapeDtypeStruct(gated_input.shape, BF),
            jax.ShapeDtypeStruct(filters.shape, F32),
        ],
        in_specs=[anywhere] * 4 + [pl.BlockSpec(memory_space=pltpu.SMEM)],
        out_specs=[pl.BlockSpec(memory_space=pltpu.VMEM)] * 3,
        scratch_shapes=[natural] * 3
        + [grouped] * 4
        + [pltpu.VMEM((ZERO // 2, 16, 128), BF)]
        + [shards] * 2
        + [pltpu.VMEM((8, 8, 128), F32), pltpu.VMEM((16, 8, 128), F32)]
        + [pltpu.VMEM((5, 8, 128), F32), pltpu.VMEM((3, 4, 8, 128), F32)]
        + [dma((2,))] * 3
        + [dma((CHUNKS,))] * 4
        + [dma((1,)), dma((3,)), dma((3,)), dma((2,)), dma((8,))],
        compiler_params=pltpu.CompilerParams(
            collective_id=0, has_side_effects=True, vmem_limit_bytes=51 << 20
        ),
        cost_estimate=pl.CostEstimate(flops=4 << 30, bytes_accessed=8 << 20, transcendentals=0),
    )(gated_input, query_gate, cotangent, shard, step_index)
    return conv, input_grad, new_filters


def solution(mesh):
    split = P("rep", "zero", None)
    return jax.shard_map(
        on_device,
        mesh=mesh,
        in_specs=(split,) * 6 + (P(),),
        out_specs=(split,) * 3,
        check_vma=False,
    )
```
